32 devices in a mesh: dp: 4 (over z), ctx: 2 (over x), tp: 4 (over y, core).
Axes of the slice: x: 2, y: 2, z: 4, core: 2. Of those that a mesh axis runs over, the one named last changes fastest.
Arguments:
- tokens: bfloat16 [8192, 1024], P(('dp', 'ctx')), may hold values from -6 to 6
- cotangent: bfloat16 [8192, 1024], P(('dp', 'ctx')), may hold values from -6 to 6
- lengths: int32 [4, 4], P('dp'), may hold values from 1 to 2048, as said below
- norm1_gain: float32 [1024], replicated, may hold values from 0.5 to 1.5
- norm2_gain: float32 [1024], replicated, may hold values from 0.5 to 1.5
- query_proj: bfloat16 [1024, 512], P(('dp', 'ctx'), 'tp'), may hold values from -0.1875 to 0.1875
- keyval_proj: bfloat16 [1024, 2, 128], P(('dp', 'ctx')), may hold values from -0.1875 to 0.1875
- attn_proj: bfloat16 [512, 1024], P('tp', ('dp', 'ctx')), may hold values from -1 to 1
- inner_proj: bfloat16 [1024, 2, 1536], P(('dp', 'ctx'), None, 'tp'), may hold values from -0.1875 to 0.1875
- state_proj: bfloat16 [1024, 2, 128], P(('dp', 'ctx')), may hold values from -0.1875 to 0.1875
- step_proj: bfloat16 [1024, 24], P(('dp', 'ctx'), 'tp'), may hold values from -0.1875 to 0.1875
- conv_inner: float32 [5, 1536], replicated, may hold values from -3 to 3
- conv_state: float32 [5, 2, 128], replicated, may hold values from -3 to 3
- step_bias: float32 [24], replicated, may hold values from -9 to -2
- decay_log: float32 [24], replicated, may hold values from -1 to 1
- skip_gain: float32 [24], replicated, may hold values from 0.5 to 1.5
- mamba_gain: float32 [1536], replicated, may hold values from 0.5 to 1.5
- mamba_proj: bfloat16 [1536, 1024], P('tp', ('dp', 'ctx')), may hold values from -0.15625 to 0.15625
- gateup_proj: bfloat16 [1024, 2, 2048], P(('dp', 'ctx'), None, 'tp'), may hold values from -0.1875 to 0.1875
- down_proj: bfloat16 [2048, 1024], P('tp', ('dp', 'ctx')), may hold values from -0.125 to 0.125
Outputs:
- layer_out: bfloat16 [8192, 1024], P(('dp', 'ctx'))
- tokens_grad: bfloat16 [8192, 1024], P(('dp', 'ctx'))
- norm1_grad: float32 [1024], replicated
- norm2_grad: float32 [1024], replicated
- query_grad: float32 [1024, 512], P(('dp', 'ctx'), 'tp')
- keyval_grad: float32 [1024, 2, 128], P(('dp', 'ctx'))
- attn_grad: float32 [512, 1024], P('tp', ('dp', 'ctx'))
- inner_grad: float32 [1024, 2, 1536], P(('dp', 'ctx'), None, 'tp')
- state_grad: float32 [1024, 2, 128], P(('dp', 'ctx'))
- step_grad: float32 [1024, 24], P(('dp', 'ctx'), 'tp')
- convin_grad: float32 [5, 1536], replicated
- convst_grad: float32 [5, 2, 128], replicated
- stepbias_grad: float32 [24], replicated
- decay_grad: float32 [24], replicated
- skip_grad: float32 [24], replicated
- mgain_grad: float32 [1536], replicated
- mamba_grad: float32 [1536, 1024], P('tp', ('dp', 'ctx'))
- gateup_grad: float32 [1024, 2, 2048], P(('dp', 'ctx'), None, 'tp')
- down_grad: float32 [2048, 1024], P('tp', ('dp', 'ctx'))
The draws below stay inside these ranges and needn't reach their ends.
Inputs may be any that keep to these rules, and one draw needn't show every extreme that they name: Row r lists, in order, the lengths of the 4 documents packed into the 2048 tokens of dp index r; each row sums to 2048.
All inputs are finite; a program needn't handle non-finite values.
Results may differ from the reference program's by a relative error of at most 0.03.
Values may be sent and summed in bfloat16 or wider, within the bound.
No kernel may reach another device: no remote copies, remote signals or barrier semaphores. Data moves between devices by JAX's collectives and lax.ppermute only.
A program may use at most 192 MiB of HBM per device.

```python
import jax
import jax.numpy as jnp
from jax import lax

D = 1024
KVH = 2
HD = 64
NH = 24
PD = 64
NST = 128
FF = 2048
CONV = 4
SCAN_BLOCK = 256
KEY_BLOCK = 512
TOK_DEV = 1024
PACK = 2048
TOKENS = 8192
QW = 512
KVW = 128
DSSM = 1536
N_DP = 4


def draw_lengths(key, part):
    key = jax.random.fold_in(key, 5)
    first_key, end_key, split_key = jax.random.split(key, 3)
    first_len = jax.random.randint(first_key, (N_DP,), 1, TOK_DEV // 2 + 1)
    long_end = jax.random.randint(end_key, (N_DP,), PACK - TOK_DEV + 1, PACK - 1)
    remain = PACK - long_end
    third_len = jax.random.randint(split_key, (N_DP,), 1, remain)
    return jnp.stack([first_len, long_end - first_len, third_len, remain - third_len], axis=1).astype(jnp.int32)


def draw_step_bias(key, part):
    key = jax.random.fold_in(key, 7)
    return jax.random.uniform(key, (NH,), jnp.float32, -7.0, -2.0)


def steps_of(own_key, extent, cuts, low, largest):
    def one(position, parts):
        steps = jax.random.uniform(jax.random.fold_in(jax.random.fold_in(own_key, 6), position), (parts,), jnp.float32, low / len(cuts), largest / len(cuts))
        return jnp.repeat(jnp.exp(steps), extent[position] // parts).reshape((-1,) + (1,) * (len(extent) - position - 1))

    level = one(*cuts[0])
    for cut in cuts[1:]:
        level = level * one(*cut)
    return level


def bell_draw(stream_key, extent, scale, bound, shards=(), held_as=jnp.bfloat16):
    values = jax.random.normal(stream_key, extent, jnp.float32) * scale
    if len(shards) > 0:
        values = steps_of(stream_key, extent, shards, -0.22, 0.18) * values
    return jnp.clip(values, min=-bound, max=bound).astype(held_as)


def setup_inputs(seed: int = 0) -> dict:
    seeds = jax.random.split(jax.random.key(seed), 21)
    return {
        "tokens": bell_draw(seeds[0], (TOKENS, D), 1.0, 6.0, ((0, 8),)),
        "cotangent": bell_draw(seeds[1], (TOKENS, D), 1.0, 6.0, ((0, 8),)),
        "lengths": draw_lengths(jax.random.fold_in(seeds[20], 71), 0),
        "norm1_gain": jnp.clip(1.0 + 0.1 * jax.random.normal(seeds[3], (D,), jnp.float32), 0.5, 1.5),
        "norm2_gain": jnp.clip(1.0 + 0.1 * jax.random.normal(seeds[4], (D,), jnp.float32), 0.5, 1.5),
        "query_proj": bell_draw(seeds[5], (D, QW), D ** -0.5, 0.1875, ((0, 8), (1, 4))),
        "keyval_proj": bell_draw(seeds[6], (D, 2, KVW), D ** -0.5, 0.1875, ((0, 8),)),
        "attn_proj": bell_draw(seeds[7], (QW, D), 32 ** -0.5, 1.0, ((0, 4), (1, 8))),
        "inner_proj": bell_draw(seeds[8], (D, 2, DSSM), D ** -0.5, 0.1875, ((0, 8), (2, 4))),
        "state_proj": bell_draw(seeds[9], (D, 2, NST), D ** -0.5, 0.1875, ((0, 8),)),
        "step_proj": bell_draw(seeds[10], (D, NH), D ** -0.5, 0.1875, ((0, 8), (1, 4))),
        "conv_inner": bell_draw(seeds[11], (CONV + 1, DSSM), 0.5, 3.0, (), jnp.float32),
        "conv_state": bell_draw(seeds[12], (CONV + 1, 2, NST), 0.5, 3.0, (), jnp.float32),
        "step_bias": draw_step_bias(jax.random.fold_in(seeds[20], 71), 0),
        "decay_log": jnp.clip(jax.random.uniform(seeds[14], (NH,), jnp.float32, -1.0, 1.0), -1.0, 1.0),
        "skip_gain": jnp.clip(jax.random.uniform(seeds[15], (NH,), jnp.float32, 0.5, 1.5), 0.5, 1.5),
        "mamba_gain": jnp.clip(1.0 + 0.1 * jax.random.normal(seeds[16], (DSSM,), jnp.float32), 0.5, 1.5),
        "mamba_proj": bell_draw(seeds[17], (DSSM, D), DSSM ** -0.5, 0.15625, ((0, 4), (1, 8))),
        "gateup_proj": bell_draw(seeds[18], (D, 2, FF), D ** -0.5, 0.1875, ((0, 8), (2, 4))),
        "down_proj": bell_draw(seeds[19], (FF, D), FF ** -0.5, 0.125, ((0, 4), (1, 8))),
    }


EPS = 1e-05
ROPE_BASE = 10000.0
MASKED = -1e+30
HIGH = lax.Precision.HIGHEST

@jax.custom_vjp
def low(v):
    return lax.optimization_barrier(v.astype(jnp.bfloat16)).astype(jnp.float32)

@jax.custom_vjp
def low_back(v):
    return v

def low_keep(v):
    return (low(v), None)

def low_pass(kept, grad):
    return (grad,)

def back_keep(v):
    return (v, None)

def back_low(kept, grad):
    return (low(grad),)
low.defvjp(low_keep, low_pass)
low_back.defvjp(back_keep, back_low)

def matmul(left, right):
    return jnp.dot(left, right, precision=HIGH, preferred_element_type=jnp.float32)

def rms_scale(values, gain):
    return values * lax.rsqrt(lax.optimization_barrier(jnp.mean(values * values, axis=-1, keepdims=True)) + EPS) * gain

def rope_turn(values, rel_pos):
    half_dim = values.shape[-1] // 2
    frequency = ROPE_BASE ** (-jnp.arange(half_dim, dtype=jnp.float32) / half_dim)
    angles = rel_pos.astype(jnp.float32)[:, None] * frequency[None, :]
    cosine = jnp.cos(angles)[:, None, :]
    sine_part = jnp.sin(angles)[:, None, :]
    first_half = values[..., :half_dim]
    second = values[..., half_dim:]
    return jnp.concatenate([first_half * cosine - second * sine_part, second * cosine + first_half * sine_part], axis=-1)

def doc_layout(doc_lengths, positions):
    bounds = jnp.cumsum(doc_lengths).astype(jnp.int32)
    doc_ids = lax.optimization_barrier(jnp.sum((positions[:, None] >= bounds[None, :]).astype(jnp.int32), axis=1)).astype(jnp.int32)
    starts = (bounds - doc_lengths).astype(jnp.int32)
    member = doc_ids[:, None] == jnp.arange(bounds.shape[0], dtype=jnp.int32)[None, :]
    doc_start = lax.optimization_barrier(jnp.sum(jnp.where(member, starts[None, :], 0), axis=1)).astype(jnp.int32)
    return (doc_ids, (positions - doc_start).astype(jnp.int32))

def causal_conv(extended, taps, rel_pos):
    width = taps.shape[0] - 1
    row_count = rel_pos.shape[0]
    summed = taps[width]
    for lag_steps in range(width):
        shifted = extended[width - 1 - lag_steps:width - 1 - lag_steps + row_count]
        summed = summed + taps[width - 1 - lag_steps] * shifted * (rel_pos >= lag_steps).astype(jnp.float32)[:, None]
    return jax.nn.silu(summed)

def scan_block(carried_in, block_in):
    state_now, state_doc = carried_in
    inner_vals, step_size, log_decay, write_vec, read_vec, doc_ids = block_in
    cumulative = jnp.cumsum(log_decay, axis=0)
    order_idx = jnp.arange(doc_ids.shape[0], dtype=jnp.int32)
    linked = (doc_ids[:, None] == doc_ids[None, :]) & (order_idx[:, None] >= order_idx[None, :])
    weights = jnp.exp(jnp.where(linked[:, :, None], cumulative[:, None, :] - cumulative[None, :, :], MASKED))
    couple = jnp.dot(read_vec, write_vec.T, precision=HIGH)
    mixing = couple[:, :, None] * weights * step_size[None, :, :]
    within = jnp.einsum('tsh,shp->thp', mixing, inner_vals, precision=HIGH)
    inflow = (doc_ids == state_doc).astype(jnp.float32)[:, None] * jnp.exp(cumulative)
    carried = jnp.einsum('tn,hpn->thp', read_vec, state_now, precision=HIGH) * inflow[:, :, None]
    last_doc = doc_ids[-1]
    tail_weight = jnp.where((doc_ids == last_doc)[:, None], jnp.exp(cumulative[-1][None, :] - cumulative), 0.0) * step_size
    kept_part = jnp.where(state_doc == last_doc, jnp.exp(cumulative[-1]), 0.0)
    new_state = kept_part[:, None, None] * state_now + jnp.einsum('sh,shp,sn->hpn', tail_weight, inner_vals, write_vec, precision=HIGH)
    return ((new_state, last_doc), within + carried)

def state_scan(inner_vals, step_size, log_decay, write_vec, read_vec, doc_ids, block_len):
    pieces = inner_vals.shape[0] // block_len

    def split_rows(values):
        return values.reshape((pieces, block_len) + values.shape[1:])
    start_state = jnp.zeros((inner_vals.shape[1], inner_vals.shape[2], write_vec.shape[1]), jnp.float32)
    blocks_in = (split_rows(inner_vals), split_rows(step_size), split_rows(log_decay), split_rows(write_vec), split_rows(read_vec), split_rows(doc_ids))
    final_pair, outputs = lax.scan(jax.checkpoint(scan_block), (start_state, jnp.array(-1, jnp.int32)), blocks_in)
    return (outputs.reshape(inner_vals.shape), final_pair[0])

def layer(hidden_in, doc_lengths, params):
    norm1_g, norm2_g, query_w, keyval_w, attn_w, inner_w, state_w, step_w, conv_in, conv_st, step_b, decay_l, skip_g, mamba_g, mamba_w, gateup_w, down_w = params
    rows_total = hidden_in.shape[0]
    positions = jnp.arange(rows_total, dtype=jnp.int32)
    doc_ids, rel_pos = doc_layout(doc_lengths, positions)
    normed = low(rms_scale(hidden_in, norm1_g))
    heads_q = query_w.shape[1] // HD
    queries = low_back(matmul(normed, query_w)).reshape(rows_total, heads_q, HD)
    q_rot = low(rope_turn(queries, rel_pos))
    keyval = low_back(matmul(normed, keyval_w.reshape(D, -1))).reshape(rows_total, 2, KVH, HD)
    k_rot = low(rope_turn(keyval[:, 0], rel_pos))
    v_low = low(keyval[:, 1])
    group_size = heads_q // KVH
    k_wide = jnp.repeat(k_rot, group_size, axis=1)
    v_wide = jnp.repeat(v_low, group_size, axis=1)
    score_scale = HD ** (-0.5)

    def attend(block_in):
        q_block, doc_block, pos_block = block_in
        scores = low_back(jnp.einsum('qhd,khd->hqk', q_block, k_wide, precision=HIGH) * score_scale)
        allowed = (doc_block[:, None] == doc_ids[None, :]) & (positions[None, :] <= pos_block[:, None])
        scores = jnp.where(allowed[None], scores, MASKED)
        probs = low(jax.nn.softmax(scores, axis=-1))
        return jnp.einsum('hqk,khd->qhd', probs, v_wide, precision=HIGH)
    blocks_in = (q_rot.reshape(-1, KEY_BLOCK, heads_q, HD), doc_ids.reshape(-1, KEY_BLOCK), positions.reshape(-1, KEY_BLOCK))
    attended = lax.map(jax.checkpoint(attend), blocks_in).reshape(rows_total, heads_q * HD)
    attn_part = matmul(low(low_back(attended)), attn_w)
    inner_all = low_back(matmul(normed, inner_w.reshape(D, -1)))
    gate_z = inner_all[:, :DSSM]
    inner_x = low(inner_all[:, DSSM:])
    state_all = low(low_back(matmul(normed, state_w.reshape(D, -1))))
    step_raw = low_back(matmul(normed, step_w))
    mixed_in = jnp.concatenate([inner_x, state_all], axis=1)
    extended = jnp.concatenate([jnp.zeros((CONV - 1, mixed_in.shape[1]), jnp.float32), mixed_in], axis=0)
    taps = jnp.concatenate([conv_in, conv_st.reshape(CONV + 1, -1)], axis=1)
    activated = causal_conv(extended, taps, rel_pos)
    inner_vals = activated[:, :DSSM].reshape(rows_total, NH, PD)
    write_vec = activated[:, DSSM:DSSM + NST]
    read_vec = activated[:, DSSM + NST:]
    step_size = jax.nn.softplus(step_raw + step_b)
    log_decay = -step_size * jnp.exp(decay_l)
    ssm_out, _final = state_scan(inner_vals, step_size, log_decay, write_vec, read_vec, doc_ids, SCAN_BLOCK)
    with_skip = ssm_out + skip_g[None, :, None] * inner_vals
    gated = with_skip * jax.nn.silu(gate_z).reshape(rows_total, NH, PD)
    normed_heads = gated * lax.rsqrt(lax.optimization_barrier(jnp.mean(gated * gated, axis=-1, keepdims=True)) + EPS) * mamba_g.reshape(NH, PD)
    mamba_part = matmul(low(normed_heads.reshape(rows_total, DSSM)), mamba_w)
    mixer_sum = low_back(attn_part + mamba_part)
    residual = hidden_in + mixer_sum
    normed2 = low(rms_scale(residual, norm2_g))
    gateup = low_back(matmul(normed2, gateup_w.reshape(D, -1)))
    hidden_act = low(jax.nn.silu(gateup[:, :FF]) * gateup[:, FF:])
    return residual + matmul(hidden_act, down_w)

def reference(tokens, cotangent, lengths, norm1_gain, norm2_gain, query_proj, keyval_proj, attn_proj, inner_proj, state_proj, step_proj, conv_inner, conv_state, step_bias, decay_log, skip_gain, mamba_gain, mamba_proj, gateup_proj, down_proj):
    params = tuple((weight.astype(jnp.float32) for weight in (norm1_gain, norm2_gain, query_proj, keyval_proj, attn_proj, inner_proj, state_proj, step_proj, conv_inner, conv_state, step_bias, decay_log, skip_gain, mamba_gain, mamba_proj, gateup_proj, down_proj)))
    packs_in = tokens.astype(jnp.float32).reshape(N_DP, -1, D)
    packs_cot = cotangent.astype(jnp.float32).reshape(N_DP, -1, D)

    def one_pack(totals, pack_data):
        pack_in, pack_cot, doc_lengths = pack_data
        result, pull_back = jax.vjp(lambda hidden_in, weights: layer(hidden_in, doc_lengths, weights), pack_in, params)
        grad_in, grad_weights = pull_back(pack_cot)
        return (jax.tree.map(jnp.add, totals, grad_weights), (result, grad_in))
    zero_grads = jax.tree.map(jnp.zeros_like, params)
    totals, (results, grads_in) = lax.scan(one_pack, zero_grads, (packs_in, packs_cot, lengths))
    g_norm1, g_norm2, g_query, g_keyval, g_attn, g_inner, g_state, g_step, g_convin, g_convst, g_stepbias, g_decay, g_skip, g_mgain, g_mamba, g_gateup, g_down = totals
    return (results.reshape(tokens.shape).astype(jnp.bfloat16), grads_in.reshape(tokens.shape).astype(jnp.bfloat16), g_norm1, g_norm2, g_query, g_keyval, g_attn, g_inner, g_state, g_step, g_convin, g_convst, g_stepbias, g_decay, g_skip, g_mgain, g_mamba, g_gateup, g_down)
```

```python
import functools

import jax
import jax.numpy as jnp
from jax import lax
from jax.experimental import pallas as pl
from jax.experimental.pallas import tpu as pltpu
from jax.sharding import PartitionSpec as P

H = 8
KVH = 2
HD = 64
PD = 64
NST = 128
CONV = 4
CHUNK = 256
QUERY_BLOCK = 256
KEY_BLOCK = 512
EDGE = 8
LANES = 128
VMEM_BYTES = 48 * 1024 * 1024

EPS = 1e-05
ROPE_BASE = 10000.0
MASKED = -1e30
HIGH = lax.Precision.HIGHEST
F32 = jnp.float32
BF16 = jnp.bfloat16
WEIGHT_AXES = ("dp", "ctx")


def product(left, right):
    return jnp.dot(left, right, preferred_element_type=F32)


def product_tn(left, right):
    return lax.dot_general(left, right, (((0,), (0,)), ((), ())), preferred_element_type=F32)


def product_nt(left, right):
    return lax.dot_general(left, right, (((1,), (1,)), ((), ())), preferred_element_type=F32)


def low_nn(left, right):
    return product(left.astype(BF16), right.astype(BF16))


def low_tn(left, right):
    return product_tn(left.astype(BF16), right.astype(BF16))


def low_nt(left, right):
    return product_nt(left.astype(BF16), right.astype(BF16))


def split_nn(left, ones):
    first = left.astype(BF16)
    second = (left - first.astype(F32)).astype(BF16)
    return product(first, ones) + product(second, ones)


def split_nt(ones, right):
    first = right.astype(BF16)
    second = (right - first.astype(F32)).astype(BF16)
    return product_nt(ones, first) + product_nt(ones, second)


def iota(shape, dim):
    return lax.broadcasted_iota(jnp.int32, shape, dim)


def start_of(rows, meta, docs):
    start = jnp.full(rows.shape, meta[0], jnp.int32)
    for doc in range(1, docs):
        start = jnp.where(rows >= meta[doc], meta[doc], start)
    return start


def start_of_one(row, meta, docs):
    start = meta[0]
    for doc in range(1, docs):
        start = jnp.where(row >= meta[doc], meta[doc], start)
    return start


def sigmoid(values):
    return 1.0 / (1.0 + jnp.exp(-values))


def swap_halves(values):
    lane = iota(values.shape, 1)
    up = pltpu.roll(values, LANES - HD // 2, 1)
    down = pltpu.roll(values, HD // 2, 1)
    return jnp.where(lane % HD < HD // 2, up, down)


def prep_kernel(
    docs,
    inner_width,
    meta,
    proj,
    edge,
    taps,
    heads,
    cosine,
    sine,
    spread,
    spread_t,
    q_out,
    kv_out,
    mixed_out,
    act_out,
    slope_out,
    step_out,
    sig_out,
    cum_out,
    state_out,
    end_out,
    ext,
    state,
    total_log,
):
    c = pl.program_id(0)
    rows = proj.shape[0]
    mix = ext.shape[1]
    row = c * rows + iota((rows, 1), 0)
    rel = row - start_of(row, meta, docs)
    mixed = proj[:, inner_width : inner_width + mix].astype(BF16)
    mixed_out[...] = mixed

    @pl.when(c == 0)
    def _():
        ext[0:EDGE] = edge[...]
        state[...] = jnp.zeros_like(state)
        total_log[...] = jnp.zeros_like(total_log)

    @pl.when(c > 0)
    def _():
        ext[0:EDGE] = ext[rows : rows + EDGE]

    ext[EDGE : EDGE + rows] = mixed.astype(F32)
    pre = jnp.broadcast_to(taps[CONV : CONV + 1, :], (rows, mix))
    for lag in range(CONV):
        keep = (rel >= lag).astype(F32)
        pre = pre + taps[CONV - 1 - lag : CONV - lag, :] * (
            ext[EDGE - lag : EDGE - lag + rows] * keep
        )
    sig = sigmoid(pre)
    act = pre * sig
    act_out[...] = act
    slope_out[...] = sig * (1.0 + pre * (1.0 - sig))

    base = inner_width + mix
    cos, sin = (cosine[...], sine[...])
    queries = proj[:, base : base + LANES]
    turned = queries * cos + swap_halves(queries) * sin
    q_out[...] = (turned * HD ** (-0.5)).astype(BF16)
    keyval = proj[:, base + LANES : base + 2 * LANES]
    is_key = iota(keyval.shape, 1) < HD
    kv_out[...] = jnp.where(is_key, keyval * cos + swap_halves(keyval) * sin, keyval).astype(BF16)

    raw = proj[:, base + 2 * LANES : base + 3 * LANES] + heads[0:1, :]
    step = jnp.maximum(raw, 0.0) + jnp.log1p(jnp.exp(-jnp.abs(raw)))
    decay = -step * heads[1:2, :]
    lower = (iota((rows, rows), 0) >= iota((rows, rows), 1)).astype(F32)
    cum = jnp.dot(lower, decay, precision=HIGH, preferred_element_type=F32)
    step_out[...] = step
    sig_out[...] = sigmoid(raw)
    cum_out[...] = cum

    last = c * rows + rows - 1
    last_start = start_of_one(last, meta, docs)
    total = cum[rows - 1 : rows, :]
    tail = jnp.where(row >= last_start, jnp.exp(total - cum), 0.0) * step
    goes_on = jnp.where(last_start < c * rows, 1.0, 0.0)
    kept = split_nt(spread_t[...], jnp.broadcast_to(jnp.exp(total) * goes_on, (NST, LANES)))
    state_out[...] = state[...]
    added = low_tn(act[:, :inner_width] * split_nn(tail, spread[...]), act[:, inner_width : inner_width + NST])
    state[...] = kept * state[...] + added
    total_log[...] = total_log[...] + jnp.broadcast_to(total, total_log.shape)

    @pl.when(c == pl.num_programs(0) - 1)
    def _():
        through = jnp.exp(total_log[0:1, :]) * jnp.where(last_start < 0, 1.0, 0.0)
        first = through.astype(BF16)
        second = (through - first.astype(F32)).astype(BF16)
        sub = iota((16, LANES), 0)
        end_out[0:inner_width] = state[...].astype(BF16)
        end_out[inner_width : inner_width + 16] = jnp.where(
            sub == 0, first.astype(F32), jnp.where(sub == 1, second.astype(F32), 0.0)
        ).astype(BF16)


def intra_kernel(docs, inner_width, meta, act, step, cum, spread, y_out):
    c = pl.program_id(0)
    rows = act.shape[0]
    row = iota((rows, 1), 0)
    first = start_of(c * rows + row, meta, docs) - c * rows
    col = iota((rows, rows), 1)
    linked = (col >= first) & (col <= iota((rows, rows), 0))
    couple = low_nt(act[:, inner_width + NST :], act[:, inner_width : inner_width + NST])
    weighted = (act[:, :inner_width] * split_nn(step[...], spread[...])).astype(BF16)
    cum_now = cum[...]
    cum_t = cum_now.T
    lane = iota((rows, LANES), 1)
    for pair in range(inner_width // LANES):
        values = weighted[:, pair * LANES : (pair + 1) * LANES]
        results = []
        for head in (2 * pair, 2 * pair + 1):
            arg = cum_now[:, head : head + 1] - cum_t[head : head + 1, :]
            mixing = couple * jnp.exp(jnp.where(linked, arg, MASKED))
            results.append(product(mixing.astype(BF16), values))
        y_out[:, pair * LANES : (pair + 1) * LANES] = jnp.where(lane < PD, results[0], results[1])


def two_heads(values, upper):
    values = values.astype(F32)
    lane = iota(values.shape, 1)
    rolled = pltpu.roll(values, HD, 1)
    keep = lane >= HD if upper else lane < HD
    pair = (rolled, values) if upper else (values, rolled)
    return jnp.concatenate([jnp.where(keep, part, 0.0) for part in pair], axis=0)


def attend_kernel(docs, meta, q, kv, out, lse_out):
    block = pl.program_id(0)
    rows = q.shape[0]
    first_row = meta[docs]
    row = block * rows + iota((rows, 1), 0)
    start = start_of(row, meta, docs)
    queries = two_heads(q[...], False).astype(BF16)
    low_block = (start_of_one(block * rows, meta, docs) + first_row) // KEY_BLOCK
    high_block = (first_row + (block + 1) * rows + KEY_BLOCK - 1) // KEY_BLOCK

    def one(index, sums):
        top, total, summed = sums
        at = pl.multiple_of(index * KEY_BLOCK, KEY_BLOCK)
        keyval = kv[pl.ds(at, KEY_BLOCK), :]
        scores = product_nt(queries, keyval)
        key = index * KEY_BLOCK - first_row + iota((rows, KEY_BLOCK), 1)
        allowed = (key >= start) & (key <= row)
        allowed = jnp.concatenate([allowed, allowed], axis=0)
        scores = jnp.where(allowed, scores, MASKED)
        new_top = jnp.maximum(top, jnp.max(scores, axis=1, keepdims=True))
        scale = jnp.exp(top - new_top)
        probs = jnp.exp(scores - new_top)
        total = total * scale + jnp.sum(probs, axis=1, keepdims=True)
        return (new_top, total, summed * scale + product(probs.astype(BF16), keyval))

    top, total, summed = lax.fori_loop(
        low_block,
        high_block,
        one,
        (
            jnp.full((2 * rows, 1), MASKED, F32),
            jnp.zeros((2 * rows, 1), F32),
            jnp.zeros((2 * rows, LANES), F32),
        ),
    )
    result = summed / total
    lse = top + jnp.log(total)
    lane = iota((rows, LANES), 1)
    out[...] = jnp.where(lane < HD, pltpu.roll(result[:rows], HD, 1), result[rows:]).astype(BF16)
    lse_out[...] = jnp.where(lane < HD, lse[:rows], lse[rows:])


def attend_back_kernel(docs, meta, q, kv, grad, att, lse, cosine, sine, gq_out, gkv_out):
    block = pl.program_id(0)
    rows = q.shape[0]
    first_row = meta[docs]

    @pl.when(block == 0)
    def _():
        gkv_out[...] = jnp.zeros_like(gkv_out)

    row = block * rows + iota((rows, 1), 0)
    start = start_of(row, meta, docs)
    queries = two_heads(q[...], False).astype(BF16)
    grads = two_heads(grad[...].astype(BF16), True)
    lse_now = lse[...]
    lse_col = jnp.concatenate([lse_now[:, 0:1], lse_now[:, HD : HD + 1]], axis=0)
    delta = jnp.sum(grads * two_heads(att[...], True), axis=1, keepdims=True)
    grads = grads.astype(BF16)
    low_block = (start_of_one(block * rows, meta, docs) + first_row) // KEY_BLOCK
    high_block = (first_row + (block + 1) * rows + KEY_BLOCK - 1) // KEY_BLOCK

    def one(index, summed):
        at = pl.multiple_of(index * KEY_BLOCK, KEY_BLOCK)
        keyval = kv[pl.ds(at, KEY_BLOCK), :]
        scores = product_nt(queries, keyval)
        key = index * KEY_BLOCK - first_row + iota((rows, KEY_BLOCK), 1)
        allowed = (key >= start) & (key <= row)
        allowed = jnp.concatenate([allowed, allowed], axis=0)
        probs = jnp.exp(jnp.where(allowed, scores - lse_col, MASKED))
        grad_scores = (probs * (product_nt(grads, keyval) - delta)).astype(BF16)
        gkv_out[pl.ds(at, KEY_BLOCK), :] += product_tn(grad_scores, queries) + product_tn(
            probs.astype(BF16), grads
        )
        return summed + product(grad_scores, keyval)

    summed = lax.fori_loop(low_block, high_block, one, jnp.zeros((2 * rows, LANES), F32))
    lane = iota((rows, LANES), 1)
    grad_q = jnp.where(lane < HD, summed[:rows], pltpu.roll(summed[rows:], HD, 1)) * HD ** (-0.5)
    gq_out[...] = (grad_q * cosine[...] - swap_halves(grad_q) * sine[...]).astype(BF16)


def finish_kernel(
    docs,
    inner_width,
    meta,
    y_in,
    act,
    cum,
    gate,
    att,
    state_local,
    state_in,
    params,
    spread,
    spread_t,
    block_ones,
    low_out,
    y_out,
    state_out,
    carry,
):
    c = pl.program_id(0)
    rows = act.shape[0]

    @pl.when(c == 0)
    def _():
        carry[...] = state_in[...]

    row = c * rows + iota((rows, 1), 0)
    start = start_of(row, meta, docs)
    last_start = start_of_one(c * rows + rows - 1, meta, docs)
    cum_now = cum[...]
    inflow = jnp.where(start < c * rows, jnp.exp(cum_now), 0.0)
    state = state_local[...] + carry[...]
    state_out[...] = state
    inner = act[:, :inner_width]
    y = y_in[...] + low_nt(act[:, inner_width + NST :], state) * split_nn(inflow, spread[...])
    y_out[...] = y
    total = jnp.exp(cum_now[rows - 1 : rows, :]) * jnp.where(last_start < c * rows, 1.0, 0.0)
    carry[...] = carry[...] * split_nt(spread_t[...], jnp.broadcast_to(total, (NST, LANES)))
    gate_now = gate[...]
    gated = (y + params[0:1, :] * inner) * (gate_now * sigmoid(gate_now))
    mean = split_nn(gated * gated, block_ones[...]) * (1.0 / PD)
    low = gated * lax.rsqrt(mean + EPS) * params[1:2, :]
    low_out[:, :LANES] = att[...]
    low_out[:, LANES:] = low.astype(BF16)


def finish_back_kernel(
    docs,
    inner_width,
    meta,
    grad,
    y_in,
    act,
    cum,
    gate,
    params,
    spread,
    block_ones,
    gy_out,
    gate_out,
    params_out,
    state_out,
    so_far,
):
    c = pl.program_id(0)
    rows = act.shape[0]

    @pl.when(c == 0)
    def _():
        params_out[...] = jnp.zeros_like(params_out)
        state_out[...] = jnp.zeros_like(state_out)
        so_far[...] = jnp.zeros_like(so_far)

    row = c * rows + iota((rows, 1), 0)
    start = start_of(row, meta, docs)
    cum_now = cum[...]
    inner = act[:, :inner_width]
    skip, gain = (params[0:1, :], params[1:2, :])
    gate_now = gate[...]
    sig = sigmoid(gate_now)
    silu = gate_now * sig
    with_skip = y_in[...] + skip * inner
    gated = with_skip * silu
    ones = block_ones[...]
    scale = lax.rsqrt(split_nn(gated * gated, ones) * (1.0 / PD) + EPS)
    grad_now = grad[...]
    unit = gated * scale
    grad_unit = grad_now * gain
    mean = split_nn(grad_unit * unit, ones) * (1.0 / PD)
    grad_gated = scale * (grad_unit - unit * mean)
    grad_y = grad_gated * silu
    gy_out[...] = grad_y
    gate_out[...] = (grad_gated * with_skip * (sig * (1.0 + gate_now * (1.0 - sig)))).astype(BF16)
    params_out[0:1, :] += jnp.sum(grad_y * inner, axis=0, keepdims=True)
    params_out[1:2, :] += jnp.sum(grad_now * unit, axis=0, keepdims=True)
    inflow = jnp.where(start < 0, jnp.exp(cum_now + so_far[0:1, :]), 0.0)
    state_out[...] += low_tn(grad_y * split_nn(inflow, spread[...]), act[:, inner_width + NST :])
    so_far[...] = so_far[...] + jnp.broadcast_to(cum_now[rows - 1 : rows, :], so_far.shape)


def scan_back_kernel(
    docs,
    inner_width,
    meta,
    act,
    slope,
    step_in,
    sig_in,
    cum,
    grad_y_in,
    state_in,
    grad_end,
    mixed,
    edge,
    taps,
    heads,
    params,
    spread,
    spread_t,
    gmix_out,
    gstep_out,
    tail_out,
    edge_out,
    taps_out,
    heads_out,
    ext,
    grad_state,
):
    c = pl.num_programs(0) - 1 - pl.program_id(0)
    rows = act.shape[0]

    @pl.when(pl.program_id(0) == 0)
    def _():
        grad_state[...] = grad_end[...]
        ext[0:EDGE] = jnp.zeros((EDGE, ext.shape[1]), F32)
        ext[EDGE + rows :] = jnp.zeros((EDGE, ext.shape[1]), F32)
        taps_out[...] = jnp.zeros_like(taps_out)
        heads_out[...] = jnp.zeros_like(heads_out)

    @pl.when(pl.program_id(0) > 0)
    def _():
        ext[EDGE + rows :] = ext[EDGE : 2 * EDGE]

    at = c * rows
    row = at + iota((rows, 1), 0)
    start = start_of(row, meta, docs)
    last_start = start_of_one(at + rows - 1, meta, docs)
    inner = act[:, :inner_width]
    write = act[:, inner_width : inner_width + NST].astype(BF16)
    read = act[:, inner_width + NST :].astype(BF16)
    step = step_in[...]
    cum_now = cum[...]
    grad_y = grad_y_in[...]
    spread_now = spread[...]
    spread_back = spread_t[...]
    state = state_in[...]
    grads = grad_state[...]
    total = cum_now[rows - 1 : rows, :]
    step_wide = split_nn(step, spread_now)
    weighted = inner * step_wide
    tail = split_nn(jnp.where(row >= last_start, jnp.exp(total - cum_now), 0.0), spread_now)
    inflow = split_nn(jnp.where(start < at, jnp.exp(cum_now), 0.0), spread_now)
    kept_row = jnp.exp(total) * jnp.where(last_start < at, 1.0, 0.0)

    grads_low = grads.astype(BF16)
    state_low = state.astype(BF16)
    from_state = tail * product_nt(write, grads_low)
    leaving = split_nn(weighted * from_state, spread_back)
    grad_write = low_nn(tail * weighted, grads_low)
    arriving_y = inflow * grad_y
    arriving_low = arriving_y.astype(BF16)
    grad_read = product(arriving_low, state_low)
    arriving = split_nn(arriving_y * product_nt(read, state_low), spread_back)
    grad_state[...] = split_nt(
        spread_back, jnp.broadcast_to(kept_row, (NST, LANES))
    ) * grads + product_tn(arriving_low, read)
    both = split_nt(jnp.ones((8, NST), BF16), grads * state)
    kept_grad = kept_row * split_nn(both, spread_back)[0:1, :]
    grad_total = kept_grad + jnp.sum(leaving, axis=0, keepdims=True)

    couple_t = product_nt(write, read)
    at_key = iota((rows, rows), 0)
    at_query = iota((rows, rows), 1)
    end_row = at + iota((1, rows), 1)
    start_row = start_of(end_row, meta, docs) - at
    linked = (at_key >= start_row) & (at_key <= at_query)
    cum_t = cum_now.T
    lane = iota((rows, LANES), 1)
    sub = iota((LANES, rows), 0)
    weighted_low = weighted.astype(BF16)
    grad_y_low = grad_y.astype(BF16)
    grad_couple = jnp.zeros((rows, rows), F32)
    grad_cum = arriving - leaving
    grad_cum_t = jnp.zeros((LANES, rows), F32)
    pieces = []
    for pair in range(inner_width // LANES):
        span = slice(pair * LANES, (pair + 1) * LANES)
        values = weighted_low[:, span]
        grads_here = grad_y_low[:, span]
        results = []
        for side in range(2):
            head = 2 * pair + side
            arg = cum_t[head : head + 1, :] - cum_now[:, head : head + 1]
            decay = jnp.exp(jnp.where(linked, arg, MASKED))
            mine = jnp.where((lane >= PD) == (side == 1), values, jnp.zeros_like(values))
            grad_mixing = product_nt(mine, grads_here) * decay
            grad_couple = grad_couple + grad_mixing
            by_log = grad_mixing * couple_t
            grad_cum = grad_cum - jnp.where(
                lane == head, jnp.sum(by_log, axis=1, keepdims=True), 0.0
            )
            grad_cum_t = grad_cum_t + jnp.where(
                sub == head, jnp.sum(by_log, axis=0, keepdims=True), 0.0
            )
            results.append(product((couple_t * decay).astype(BF16), grads_here))
        pieces.append(jnp.where(lane < PD, results[0], results[1]))
    grad_weighted = jnp.concatenate(pieces, axis=1) + from_state
    grad_couple_low = grad_couple.astype(BF16)
    grad_write = grad_write + product(grad_couple_low, read)
    grad_read = grad_read + product_tn(grad_couple_low, write)

    grad_cum = grad_cum + grad_cum_t.T
    upper = (at_query >= at_key).astype(F32)
    grad_decay = (
        jnp.dot(upper, grad_cum, precision=HIGH, preferred_element_type=F32) + grad_total
    )
    rate = heads[1:2, :]
    grad_inner = grad_weighted * step_wide + grad_y * params[0:1, :]
    grad_step = split_nn(grad_weighted * inner, spread_back) - grad_decay * rate
    grad_raw = grad_step * sig_in[...]
    gstep_out[...] = grad_raw.astype(BF16)
    heads_out[0:1, :] += jnp.sum(grad_raw, axis=0, keepdims=True)
    heads_out[1:2, :] += jnp.sum(grad_decay * (-step * rate), axis=0, keepdims=True)

    grad_pre = jnp.concatenate([grad_inner, grad_write, grad_read], axis=1) * slope[...]
    ext[EDGE : EDGE + rows] = grad_pre
    taps_out[CONV : CONV + 1, :] += jnp.sum(grad_pre, axis=0, keepdims=True)
    mixed_now = mixed[...].astype(F32)
    grad_mixed = jnp.zeros_like(grad_pre)
    for lag in range(CONV):
        target = row + lag
        keep = (target - start_of(target, meta, docs) >= lag).astype(F32)
        moved = ext[EDGE + lag : EDGE + lag + rows] * keep
        grad_mixed = grad_mixed + taps[CONV - 1 - lag : CONV - lag, :] * moved
        taps_out[CONV - 1 - lag : CONV - lag, :] += jnp.sum(
            moved * mixed_now, axis=0, keepdims=True
        )
    gmix_out[...] = grad_mixed.astype(BF16)

    @pl.when(pl.program_id(0) == 0)
    def _():
        tail_out[...] = grad_mixed[rows - EDGE :]

    @pl.when(c == 0)
    def _():
        before = iota((EDGE, 1), 0) - EDGE
        edge_now = edge[...]
        grad_edge = jnp.zeros_like(edge_now)
        for lag in range(1, CONV):
            target = before + lag
            keep = (target - start_of(target, meta, docs) >= lag).astype(F32)
            moved = ext[lag : lag + EDGE] * keep
            grad_edge = grad_edge + taps[CONV - 1 - lag : CONV - lag, :] * moved
            taps_out[CONV - 1 - lag : CONV - lag, :] += jnp.sum(
                moved * edge_now, axis=0, keepdims=True
            )
        edge_out[...] = grad_edge


def call(kernel, grid, ins, outs, scratch=()):
    def spec(shape, block, index):
        if block == "smem":
            return pl.BlockSpec(memory_space=pltpu.SMEM)
        if block is None:
            return pl.BlockSpec(shape, lambda i: (0,) * len(shape))
        return pl.BlockSpec(block, index)

    return pl.pallas_call(
        kernel,
        grid=(grid,),
        in_specs=[spec(a.shape, block, index) for a, block, index in ins],
        out_specs=[spec(shape, block, index) for shape, _, block, index in outs],
        out_shape=[jax.ShapeDtypeStruct(shape, kind) for shape, kind, _, _ in outs],
        scratch_shapes=list(scratch),
        compiler_params=pltpu.CompilerParams(
            dimension_semantics=("arbitrary",), vmem_limit_bytes=VMEM_BYTES
        ),
    )(*[a for a, _, _ in ins])


def by_row(i):
    return (i, 0)


def chain(gathered, order, width, heads, reached):
    state = jnp.zeros((width, NST), F32)
    for k in order:
        own = gathered[k, :width].astype(F32)
        through = gathered[k, width].astype(F32) + gathered[k, width + 1].astype(F32)
        wide = jnp.repeat(through[:heads], PD)[:, None]
        state = jnp.where(reached(k), wide * state + own, state)
    return state


def rms_scale(values, gain):
    return values * lax.rsqrt(jnp.mean(values * values, axis=-1, keepdims=True) + EPS) * gain


def rms_back(values, gain, grad):
    scale = lax.rsqrt(jnp.mean(values * values, axis=-1, keepdims=True) + EPS)
    unit = values * scale
    inner = jnp.mean(grad * gain * values, axis=-1, keepdims=True)
    return (scale * (grad * gain - values * scale * scale * inner), jnp.sum(grad * unit, axis=0))


def body(
    tokens,
    cotangent,
    lengths,
    norm1_gain,
    norm2_gain,
    query_proj,
    keyval_proj,
    attn_proj,
    inner_proj,
    state_proj,
    step_proj,
    conv_inner,
    conv_state,
    step_bias,
    decay_log,
    skip_gain,
    mamba_gain,
    mamba_proj,
    gateup_proj,
    down_proj,
):
    rows = tokens.shape[0]
    rank = lax.axis_index("tp")
    ranks = lax.axis_size("tp")
    ctx_rank = lax.axis_index("ctx")
    ctx_size = lax.axis_size("ctx")
    pack = rows * ctx_size
    shard = query_proj.shape[0]
    width = inner_proj.shape[2]
    heads = width // PD
    mix = width + 2 * NST
    ff = gateup_proj.shape[2]
    docs = lengths.shape[1]
    quarter = rows // ranks
    chunks = rows // CHUNK
    kv_head = rank * (query_proj.shape[1] // HD) // (H // KVH)

    kv_shard = lax.dynamic_slice_in_dim(keyval_proj, kv_head * HD, HD, 2).reshape(shard, 2 * HD)
    step_shard = jnp.pad(step_proj, ((0, 0), (0, LANES - heads)))
    first_shard = jnp.concatenate(
        [
            inner_proj.reshape(shard, 2 * width),
            state_proj.reshape(shard, 2 * NST),
            query_proj,
            kv_shard,
            step_shard,
        ],
        axis=1,
    )
    mixer_shard = jnp.concatenate([attn_proj.T, mamba_proj.T], axis=1)
    first_w = lax.all_gather(first_shard, WEIGHT_AXES, axis=0, tiled=True)
    mixer_w = lax.all_gather(mixer_shard, WEIGHT_AXES, axis=0, tiled=True)
    gateup_w = lax.all_gather(
        gateup_proj.reshape(shard, 2 * ff), WEIGHT_AXES, axis=0, tiled=True
    )
    down_w = lax.all_gather(down_proj.T, WEIGHT_AXES, axis=0, tiled=True)

    first_row = ctx_rank * rows
    bounds = jnp.cumsum(lengths[0])
    starts = bounds - lengths[0] - first_row
    meta = jnp.concatenate([starts, first_row[None]]).astype(jnp.int32)
    local = jnp.arange(rows, dtype=jnp.int32)
    doc_start = jnp.max(
        jnp.where(local[:, None] >= starts[None, :], starts[None, :], starts[0]), axis=1
    )
    frequency = ROPE_BASE ** (-jnp.arange(HD // 2, dtype=F32) / (HD // 2))
    angles = (local - doc_start).astype(F32)[:, None] * jnp.tile(frequency, 4)[None, :]
    sign = jnp.where(jnp.arange(LANES) % HD < HD // 2, -1.0, 1.0).astype(F32)
    cosine = jnp.cos(angles)
    sine = jnp.sin(angles) * sign[None, :]

    def mine(values, size, axis):
        return lax.dynamic_slice_in_dim(values, rank * size, size, axis)

    taps = jnp.concatenate([mine(conv_inner, width, 1), conv_state.reshape(CONV + 1, -1)], axis=1)
    taps = jnp.pad(taps, ((0, 8 - (CONV + 1)), (0, 0)))
    bias = mine(step_bias, heads, 0)
    rate = jnp.exp(mine(decay_log, heads, 0))
    head_params = jnp.pad(jnp.stack([bias, rate]), ((0, 6), (0, LANES - heads)))
    params = jnp.pad(
        jnp.stack([jnp.repeat(mine(skip_gain, heads, 0), PD), mine(mamba_gain, width, 0)]),
        ((0, 6), (0, 0)),
    )
    channel_head = jnp.arange(width) // PD
    spread = (jnp.arange(LANES)[:, None] == channel_head[None, :]).astype(BF16)
    spread_t = spread.T
    block_ones = (channel_head[:, None] == channel_head[None, :]).astype(BF16)

    hidden_in = tokens.astype(F32)
    normed = rms_scale(hidden_in, norm1_gain).astype(BF16)
    onward = [(source, source + 1) for source in range(ctx_size - 1)]
    backward = [(source + 1, source) for source in range(ctx_size - 1)]
    edge_tokens = lax.ppermute(tokens[rows - EDGE :], "ctx", onward).astype(F32)
    edge_normed = rms_scale(edge_tokens, norm1_gain).astype(BF16)
    proj = product(normed, first_w)
    edge = product(edge_normed, first_w[:, width : width + mix]).astype(BF16).astype(F32)

    chunk_128 = (CHUNK, LANES)
    chunk_mix = (CHUNK, mix)
    chunk_width = (CHUNK, width)
    q_rot, kv_local, mixed, act, slope, step, sig, cum, state_local, end = call(
        functools.partial(prep_kernel, docs, width),
        chunks,
        [
            (meta, "smem", None),
            (proj, (CHUNK, proj.shape[1]), by_row),
            (edge, None, None),
            (taps, None, None),
            (head_params, None, None),
            (cosine, chunk_128, by_row),
            (sine, chunk_128, by_row),
            (spread, None, None),
            (spread_t, None, None),
        ],
        [
            ((rows, LANES), BF16, chunk_128, by_row),
            ((rows, LANES), BF16, chunk_128, by_row),
            ((rows, mix), BF16, chunk_mix, by_row),
            ((rows, mix), F32, chunk_mix, by_row),
            ((rows, mix), F32, chunk_mix, by_row),
            ((rows, LANES), F32, chunk_128, by_row),
            ((rows, LANES), F32, chunk_128, by_row),
            ((rows, LANES), F32, chunk_128, by_row),
            ((chunks * width, NST), F32, (width, NST), by_row),
            ((width + 16, NST), BF16, None, None),
        ],
        [
            pltpu.VMEM((CHUNK + EDGE, mix), F32),
            pltpu.VMEM((width, NST), F32),
            pltpu.VMEM((8, LANES), F32),
        ],
    )
    kv_all = lax.all_gather(kv_local, "ctx", axis=0, tiled=True)
    ends = lax.all_gather(end, "ctx")
    (y_intra,) = call(
        functools.partial(intra_kernel, docs, width),
        chunks,
        [
            (meta, "smem", None),
            (act, chunk_mix, by_row),
            (step, chunk_128, by_row),
            (cum, chunk_128, by_row),
            (spread, None, None),
        ],
        [((rows, width), F32, chunk_width, by_row)],
    )
    blocks = rows // QUERY_BLOCK
    block_128 = (QUERY_BLOCK, LANES)
    attended, lse = call(
        functools.partial(attend_kernel, docs),
        blocks,
        [(meta, "smem", None), (q_rot, block_128, by_row), (kv_all, None, None)],
        [((rows, LANES), BF16, block_128, by_row), ((rows, LANES), F32, block_128, by_row)],
    )
    state_in = chain(ends, range(ctx_size - 1), width, heads, lambda k: k < ctx_rank)
    mixer_low, y, states = call(
        functools.partial(finish_kernel, docs, width),
        chunks,
        [
            (meta, "smem", None),
            (y_intra, chunk_width, by_row),
            (act, chunk_mix, by_row),
            (cum, chunk_128, by_row),
            (proj, chunk_width, by_row),
            (attended, chunk_128, by_row),
            (state_local, (width, NST), by_row),
            (state_in, None, None),
            (params, None, None),
            (spread, None, None),
            (spread_t, None, None),
            (block_ones, None, None),
        ],
        [
            ((rows, LANES + width), BF16, (CHUNK, LANES + width), by_row),
            ((rows, width), F32, chunk_width, by_row),
            ((chunks * width, NST), F32, (width, NST), by_row),
        ],
        [pltpu.VMEM((width, NST), F32)],
    )

    def scatter_rows(values):
        return lax.psum_scatter(
            values.astype(BF16), "tp", scatter_dimension=0, tiled=True
        ).astype(F32)

    def gather_rows(values):
        return lax.all_gather(values, "tp", axis=0, tiled=True)

    hidden_q = mine(hidden_in, quarter, 0)
    residual = hidden_q + scatter_rows(product_nt(mixer_low, mixer_w))
    normed2 = gather_rows(rms_scale(residual, norm2_gain).astype(BF16))
    gateup = product(normed2, gateup_w)
    gate, up = (gateup[:, :ff], gateup[:, ff:])
    gate_sig = jax.nn.sigmoid(gate)
    gate_silu = gate * gate_sig
    hidden_act = (gate_silu * up).astype(BF16)
    grad_hidden = product(cotangent, down_w)
    grad_gateup = jnp.concatenate(
        [grad_hidden * up * (gate_sig * (1.0 + gate * (1.0 - gate_sig))), grad_hidden * gate_silu],
        axis=1,
    ).astype(BF16)
    grad_norm2 = scatter_rows(product_nt(grad_gateup, gateup_w))
    grad_values, norm2_part = rms_back(residual, norm2_gain, grad_norm2)
    grad_residual = mine(cotangent, quarter, 0).astype(F32) + grad_values
    grad_mix = gather_rows(grad_residual.astype(BF16))
    layer_q = residual + scatter_rows(product_nt(hidden_act, down_w))
    layer_out = gather_rows(layer_q.astype(BF16))

    def to_owner(values):
        return lax.psum_scatter(
            values.astype(BF16), WEIGHT_AXES, scatter_dimension=0, tiled=True
        ).astype(F32)

    gateup_grad = to_owner(product_tn(normed2, grad_gateup)).reshape(gateup_proj.shape)
    down_grad = to_owner(product_tn(cotangent, hidden_act)).T

    grad_mixer = product(grad_mix, mixer_w)
    mixer_grad = to_owner(product_tn(grad_mix, mixer_low))
    attn_grad = mixer_grad[:, :LANES].T
    mamba_grad = mixer_grad[:, LANES:].T
    grad_att = grad_mixer[:, :LANES]
    grad_mamba = grad_mixer[:, LANES:]
    grad_y, grad_gate, params_grad, grad_in = call(
        functools.partial(finish_back_kernel, docs, width),
        chunks,
        [
            (meta, "smem", None),
            (grad_mamba, chunk_width, by_row),
            (y, chunk_width, by_row),
            (act, chunk_mix, by_row),
            (cum, chunk_128, by_row),
            (proj, chunk_width, by_row),
            (params, None, None),
            (spread, None, None),
            (block_ones, None, None),
        ],
        [
            ((rows, width), F32, chunk_width, by_row),
            ((rows, width), BF16, chunk_width, by_row),
            ((8, width), F32, None, None),
            ((width, NST), F32, None, None),
        ],
        [pltpu.VMEM((8, LANES), F32)],
    )
    grad_ins = lax.all_gather(
        jnp.concatenate([grad_in.astype(BF16), end[width:]], axis=0), "ctx"
    )
    grad_query, grad_kv = call(
        functools.partial(attend_back_kernel, docs),
        blocks,
        [
            (meta, "smem", None),
            (q_rot, block_128, by_row),
            (kv_all, None, None),
            (grad_att, block_128, by_row),
            (attended, block_128, by_row),
            (lse, block_128, by_row),
            (cosine, block_128, by_row),
            (sine, block_128, by_row),
        ],
        [
            ((rows, LANES), BF16, block_128, by_row),
            ((pack, LANES), F32, None, None),
        ],
    )
    grad_kv = lax.psum_scatter(
        grad_kv.astype(BF16), "ctx", scatter_dimension=0, tiled=True
    ).astype(F32)
    grad_end = chain(
        grad_ins, range(ctx_size - 1, 0, -1), width, heads, lambda k: k > ctx_rank
    )

    def back_row(i):
        return (chunks - 1 - i, 0)

    grad_mixed, grad_step, grad_tail, grad_edge, taps_grad, heads_grad = call(
        functools.partial(scan_back_kernel, docs, width),
        chunks,
        [
            (meta, "smem", None),
            (act, chunk_mix, back_row),
            (slope, chunk_mix, back_row),
            (step, chunk_128, back_row),
            (sig, chunk_128, back_row),
            (cum, chunk_128, back_row),
            (grad_y, chunk_width, back_row),
            (states, (width, NST), back_row),
            (grad_end, None, None),
            (mixed, chunk_mix, back_row),
            (edge, None, None),
            (taps, None, None),
            (head_params, None, None),
            (params, None, None),
            (spread, None, None),
            (spread_t, None, None),
        ],
        [
            ((rows, mix), BF16, chunk_mix, back_row),
            ((rows, LANES), BF16, chunk_128, back_row),
            ((EDGE, mix), F32, None, None),
            ((EDGE, mix), F32, None, None),
            ((8, mix), F32, None, None),
            ((8, LANES), F32, None, None),
        ],
        [pltpu.VMEM((CHUNK + 2 * EDGE, mix), F32), pltpu.VMEM((width, NST), F32)],
    )
    edge_grad = lax.ppermute(grad_edge, "ctx", backward)
    grad_mixed = lax.dynamic_update_slice_in_dim(
        grad_mixed, (grad_tail + edge_grad).astype(BF16), rows - EDGE, 0
    )
    half = HD // 2
    swapped = jnp.concatenate([grad_kv[:, half:HD], grad_kv[:, :half], grad_kv[:, HD:]], axis=1)
    is_key = jnp.arange(LANES)[None, :] < HD
    grad_kv = jnp.where(is_key, grad_kv * cosine - swapped * sine, grad_kv).astype(BF16)

    grad_all = jnp.concatenate([grad_gate, grad_mixed, grad_query, grad_kv, grad_step], axis=1)
    grad_norm1 = scatter_rows(product_nt(grad_all, first_w))
    grad_values, norm1_part = rms_back(hidden_q, norm1_gain, grad_norm1)
    tokens_grad = gather_rows((grad_residual + grad_values).astype(BF16))
    first_grad = to_owner(product_tn(normed, grad_all))
    inner_grad = first_grad[:, : 2 * width].reshape(inner_proj.shape)
    base = width + mix
    query_grad = first_grad[:, base : base + LANES]
    step_grad = first_grad[:, base + 2 * LANES : base + 2 * LANES + heads]
    kv_wide = lax.dynamic_update_slice_in_dim(
        jnp.zeros(keyval_proj.shape, F32),
        first_grad[:, base + LANES : base + 2 * LANES].reshape(shard, 2, HD),
        kv_head * HD,
        2,
    )
    shared = jnp.concatenate(
        [kv_wide.reshape(shard, -1), first_grad[:, 2 * width : base]], axis=1
    )
    shared = lax.psum(shared, "tp")
    keyval_grad = shared[:, : 2 * KVH * HD].reshape(keyval_proj.shape)
    state_grad = shared[:, 2 * KVH * HD :].reshape(state_proj.shape)

    def spread_out(values, full_shape, size, axis):
        return lax.dynamic_update_slice_in_dim(
            jnp.zeros(full_shape, F32), values, rank * size, axis
        )

    small = lax.psum(
        (
            norm1_part,
            norm2_part,
            spread_out(taps_grad[: CONV + 1, :width], conv_inner.shape, width, 1),
            taps_grad[: CONV + 1, width:].reshape(conv_state.shape),
            spread_out(heads_grad[0, :heads], step_bias.shape, heads, 0),
            spread_out(heads_grad[1, :heads], decay_log.shape, heads, 0),
            spread_out(
                jnp.sum(params_grad[0].reshape(heads, PD), axis=1), skip_gain.shape, heads, 0
            ),
            spread_out(params_grad[1], mamba_gain.shape, width, 0),
        ),
        ("dp", "ctx", "tp"),
    )
    return (
        layer_out,
        tokens_grad,
        small[0],
        small[1],
        query_grad,
        keyval_grad,
        attn_grad,
        inner_grad,
        state_grad,
        step_grad,
        small[2],
        small[3],
        small[4],
        small[5],
        small[6],
        small[7],
        mamba_grad,
        gateup_grad,
        down_grad,
    )


def solution(mesh):
    rows_split = P(("dp", "ctx"), None)
    split_0 = P(("dp", "ctx"), "tp")
    split_0_whole = P(("dp", "ctx"), None, None)
    split_0_last = P(("dp", "ctx"), None, "tp")
    split_1 = P("tp", ("dp", "ctx"))
    return jax.shard_map(
        body,
        mesh=mesh,
        in_specs=(
            rows_split,
            rows_split,
            P("dp", None),
            P(),
            P(),
            split_0,
            split_0_whole,
            split_1,
            split_0_last,
            split_0_whole,
            split_0,
            P(),
            P(),
            P(),
            P(),
            P(),
            P(),
            split_1,
            split_0_last,
            split_1,
        ),
        out_specs=(
            rows_split,
            rows_split,
            P(),
            P(),
            split_0,
            split_0_whole,
            split_1,
            split_0_last,
            split_0_whole,
            split_0,
            P(),
            P(),
            P(),
            P(),
            P(),
            P(),
            split_1,
            split_0_last,
            split_1,
        ),
        check_vma=False,
    )
```

```python
import functools

import jax
import jax.numpy as jnp
from jax import lax
from jax.experimental import pallas as pl
from jax.experimental.pallas import tpu as pltpu
from jax.sharding import PartitionSpec as P

H = 8
KVH = 2
HD = 64
PD = 64
NST = 128
CONV = 4
CHUNK = 256
QUERY_BLOCK = 256
KEY_BLOCK = 512
EDGE = 8
LANES = 128
VMEM_BYTES = 48 * 1024 * 1024

EPS = 1e-05
ROPE_BASE = 10000.0
MASKED = -1e30
HIGH = lax.Precision.HIGHEST
F32 = jnp.float32
BF16 = jnp.bfloat16
WEIGHT_AXES = ("dp", "ctx")


def product(left, right):
    return jnp.dot(left, right, preferred_element_type=F32)


def product_tn(left, right):
    return lax.dot_general(left, right, (((0,), (0,)), ((), ())), preferred_element_type=F32)


def product_nt(left, right):
    return lax.dot_general(left, right, (((1,), (1,)), ((), ())), preferred_element_type=F32)


def low_nn(left, right):
    return product(left.astype(BF16), right.astype(BF16))


def low_tn(left, right):
    return product_tn(left.astype(BF16), right.astype(BF16))


def low_nt(left, right):
    return product_nt(left.astype(BF16), right.astype(BF16))


def split_nn(left, ones):
    first = left.astype(BF16)
    second = (left - first.astype(F32)).astype(BF16)
    return product(first, ones) + product(second, ones)


def split_nt(ones, right):
    first = right.astype(BF16)
    second = (right - first.astype(F32)).astype(BF16)
    return product_nt(ones, first) + product_nt(ones, second)


def iota(shape, dim):
    return lax.broadcasted_iota(jnp.int32, shape, dim)


def start_of(rows, meta, docs):
    start = jnp.full(rows.shape, meta[0], jnp.int32)
    for doc in range(1, docs):
        start = jnp.where(rows >= meta[doc], meta[doc], start)
    return start


def start_of_one(row, meta, docs):
    start = meta[0]
    for doc in range(1, docs):
        start = jnp.where(row >= meta[doc], meta[doc], start)
    return start


def sigmoid(values):
    return 1.0 / (1.0 + jnp.exp(-values))


def swap_halves(values):
    lane = iota(values.shape, 1)
    up = pltpu.roll(values, LANES - HD // 2, 1)
    down = pltpu.roll(values, HD // 2, 1)
    return jnp.where(lane % HD < HD // 2, up, down)


def prep_kernel(
    docs,
    inner_width,
    meta,
    proj,
    edge,
    taps,
    heads,
    cosine,
    sine,
    spread,
    spread_t,
    q_out,
    kv_out,
    mixed_out,
    act_out,
    slope_out,
    step_out,
    sig_out,
    cum_out,
    state_out,
    end_out,
    ext,
    state,
    total_log,
):
    c = pl.program_id(0)
    rows = proj.shape[0]
    mix = ext.shape[1]
    row = c * rows + iota((rows, 1), 0)
    rel = row - start_of(row, meta, docs)
    mixed = proj[:, inner_width : inner_width + mix].astype(BF16)
    mixed_out[...] = mixed

    @pl.when(c == 0)
    def _():
        ext[0:EDGE] = edge[...]
        state[...] = jnp.zeros_like(state)
        total_log[...] = jnp.zeros_like(total_log)

    @pl.when(c > 0)
    def _():
        ext[0:EDGE] = ext[rows : rows + EDGE]

    ext[EDGE : EDGE + rows] = mixed.astype(F32)
    pre = jnp.broadcast_to(taps[CONV : CONV + 1, :], (rows, mix))
    for lag in range(CONV):
        keep = (rel >= lag).astype(F32)
        pre = pre + taps[CONV - 1 - lag : CONV - lag, :] * (
            ext[EDGE - lag : EDGE - lag + rows] * keep
        )
    sig = sigmoid(pre)
    act = pre * sig
    act_out[...] = act
    slope_out[...] = sig * (1.0 + pre * (1.0 - sig))

    base = inner_width + mix
    cos, sin = (cosine[...], sine[...])
    queries = proj[:, base : base + LANES]
    turned = queries * cos + swap_halves(queries) * sin
    q_out[...] = (turned * HD ** (-0.5)).astype(BF16)
    keyval = proj[:, base + LANES : base + 2 * LANES]
    is_key = iota(keyval.shape, 1) < HD
    kv_out[...] = jnp.where(is_key, keyval * cos + swap_halves(keyval) * sin, keyval).astype(BF16)

    raw = proj[:, base + 2 * LANES : base + 3 * LANES] + heads[0:1, :]
    step = jnp.maximum(raw, 0.0) + jnp.log1p(jnp.exp(-jnp.abs(raw)))
    decay = -step * heads[1:2, :]
    lower = (iota((rows, rows), 0) >= iota((rows, rows), 1)).astype(F32)
    cum = jnp.dot(lower, decay, precision=HIGH, preferred_element_type=F32)
    step_out[...] = step
    sig_out[...] = sigmoid(raw)
    cum_out[...] = cum

    last = c * rows + rows - 1
    last_start = start_of_one(last, meta, docs)
    total = cum[rows - 1 : rows, :]
    tail = jnp.where(row >= last_start, jnp.exp(total - cum), 0.0) * step
    goes_on = jnp.where(last_start < c * rows, 1.0, 0.0)
    kept = split_nt(spread_t[...], jnp.broadcast_to(jnp.exp(total) * goes_on, (NST, LANES)))
    state_out[...] = state[...]
    added = low_tn(act[:, :inner_width] * split_nn(tail, spread[...]), act[:, inner_width : inner_width + NST])
    state[...] = kept * state[...] + added
    total_log[...] = total_log[...] + jnp.broadcast_to(total, total_log.shape)

    @pl.when(c == pl.num_programs(0) - 1)
    def _():
        through = jnp.exp(total_log[0:1, :]) * jnp.where(last_start < 0, 1.0, 0.0)
        first = through.astype(BF16)
        second = (through - first.astype(F32)).astype(BF16)
        sub = iota((16, LANES), 0)
        end_out[0:inner_width] = state[...].astype(BF16)
        end_out[inner_width : inner_width + 16] = jnp.where(
            sub == 0, first.astype(F32), jnp.where(sub == 1, second.astype(F32), 0.0)
        ).astype(BF16)


def intra_kernel(docs, inner_width, meta, act, step, cum, spread, y_out):
    c = pl.program_id(0)
    rows = act.shape[0]
    row = iota((rows, 1), 0)
    first = start_of(c * rows + row, meta, docs) - c * rows
    col = iota((rows, rows), 1)
    linked = (col >= first) & (col <= iota((rows, rows), 0))
    couple = low_nt(act[:, inner_width + NST :], act[:, inner_width : inner_width + NST])
    weighted = (act[:, :inner_width] * split_nn(step[...], spread[...])).astype(BF16)
    cum_now = cum[...]
    cum_t = cum_now.T
    lane = iota((rows, LANES), 1)
    for pair in range(inner_width // LANES):
        values = weighted[:, pair * LANES : (pair + 1) * LANES]
        results = []
        for head in (2 * pair, 2 * pair + 1):
            arg = cum_now[:, head : head + 1] - cum_t[head : head + 1, :]
            mixing = couple * jnp.exp(jnp.where(linked, arg, MASKED))
            results.append(product(mixing.astype(BF16), values))
        y_out[:, pair * LANES : (pair + 1) * LANES] = jnp.where(lane < PD, results[0], results[1])


def two_heads(values, upper):
    values = values.astype(F32)
    lane = iota(values.shape, 1)
    rolled = pltpu.roll(values, HD, 1)
    keep = lane >= HD if upper else lane < HD
    pair = (rolled, values) if upper else (values, rolled)
    return jnp.concatenate([jnp.where(keep, part, 0.0) for part in pair], axis=0)


def attend_kernel(docs, meta, q, kv, out, lse_out):
    block = pl.program_id(0)
    rows = q.shape[0]
    first_row = meta[docs]
    row = block * rows + iota((rows, 1), 0)
    start = start_of(row, meta, docs)
    queries = two_heads(q[...], False).astype(BF16)
    low_block = (start_of_one(block * rows, meta, docs) + first_row) // KEY_BLOCK
    high_block = (first_row + (block + 1) * rows + KEY_BLOCK - 1) // KEY_BLOCK

    def one(index, sums):
        top, total, summed = sums
        at = pl.multiple_of(index * KEY_BLOCK, KEY_BLOCK)
        keyval = kv[pl.ds(at, KEY_BLOCK), :]
        scores = product_nt(queries, keyval)
        key = index * KEY_BLOCK - first_row + iota((rows, KEY_BLOCK), 1)
        allowed = (key >= start) & (key <= row)
        allowed = jnp.concatenate([allowed, allowed], axis=0)
        scores = jnp.where(allowed, scores, MASKED)
        new_top = jnp.maximum(top, jnp.max(scores, axis=1, keepdims=True))
        scale = jnp.exp(top - new_top)
        probs = jnp.exp(scores - new_top)
        total = total * scale + jnp.sum(probs, axis=1, keepdims=True)
        return (new_top, total, summed * scale + product(probs.astype(BF16), keyval))

    top, total, summed = lax.fori_loop(
        low_block,
        high_block,
        one,
        (
            jnp.full((2 * rows, 1), MASKED, F32),
            jnp.zeros((2 * rows, 1), F32),
            jnp.zeros((2 * rows, LANES), F32),
        ),
    )
    result = summed / total
    lse = top + jnp.log(total)
    lane = iota((rows, LANES), 1)
    out[...] = jnp.where(lane < HD, pltpu.roll(result[:rows], HD, 1), result[rows:]).astype(BF16)
    lse_out[...] = jnp.where(lane < HD, lse[:rows], lse[rows:])


def attend_back_kernel(docs, meta, q, kv, grad, att, lse, cosine, sine, gq_out, gkv_out):
    block = pl.program_id(0)
    rows = q.shape[0]
    first_row = meta[docs]

    @pl.when(block == 0)
    def _():
        gkv_out[...] = jnp.zeros_like(gkv_out)

    row = block * rows + iota((rows, 1), 0)
    start = start_of(row, meta, docs)
    queries = two_heads(q[...], False).astype(BF16)
    grads = two_heads(grad[...].astype(BF16), True)
    lse_now = lse[...]
    lse_col = jnp.concatenate([lse_now[:, 0:1], lse_now[:, HD : HD + 1]], axis=0)
    delta = jnp.sum(grads * two_heads(att[...], True), axis=1, keepdims=True)
    grads = grads.astype(BF16)
    low_block = (start_of_one(block * rows, meta, docs) + first_row) // KEY_BLOCK
    high_block = (first_row + (block + 1) * rows + KEY_BLOCK - 1) // KEY_BLOCK

    def one(index, summed):
        at = pl.multiple_of(index * KEY_BLOCK, KEY_BLOCK)
        keyval = kv[pl.ds(at, KEY_BLOCK), :]
        scores = product_nt(queries, keyval)
        key = index * KEY_BLOCK - first_row + iota((rows, KEY_BLOCK), 1)
        allowed = (key >= start) & (key <= row)
        allowed = jnp.concatenate([allowed, allowed], axis=0)
        probs = jnp.exp(jnp.where(allowed, scores - lse_col, MASKED))
        grad_scores = (probs * (product_nt(grads, keyval) - delta)).astype(BF16)
        gkv_out[pl.ds(at, KEY_BLOCK), :] += product_tn(grad_scores, queries) + product_tn(
            probs.astype(BF16), grads
        )
        return summed + product(grad_scores, keyval)

    summed = lax.fori_loop(low_block, high_block, one, jnp.zeros((2 * rows, LANES), F32))
    lane = iota((rows, LANES), 1)
    grad_q = jnp.where(lane < HD, summed[:rows], pltpu.roll(summed[rows:], HD, 1)) * HD ** (-0.5)
    gq_out[...] = (grad_q * cosine[...] - swap_halves(grad_q) * sine[...]).astype(BF16)


def finish_kernel(
    docs,
    inner_width,
    meta,
    y_in,
    act,
    cum,
    gate,
    att,
    state_local,
    state_in,
    params,
    spread,
    spread_t,
    block_ones,
    low_out,
    y_out,
    state_out,
    carry,
):
    c = pl.program_id(0)
    rows = act.shape[0]

    @pl.when(c == 0)
    def _():
        carry[...] = state_in[...]

    row = c * rows + iota((rows, 1), 0)
    start = start_of(row, meta, docs)
    last_start = start_of_one(c * rows + rows - 1, meta, docs)
    cum_now = cum[...]
    inflow = jnp.where(start < c * rows, jnp.exp(cum_now), 0.0)
    state = state_local[...] + carry[...]
    state_out[...] = state
    inner = act[:, :inner_width]
    y = y_in[...] + low_nt(act[:, inner_width + NST :], state) * split_nn(inflow, spread[...])
    y_out[...] = y
    total = jnp.exp(cum_now[rows - 1 : rows, :]) * jnp.where(last_start < c * rows, 1.0, 0.0)
    carry[...] = carry[...] * split_nt(spread_t[...], jnp.broadcast_to(total, (NST, LANES)))
    gate_now = gate[...]
    gated = (y + params[0:1, :] * inner) * (gate_now * sigmoid(gate_now))
    mean = split_nn(gated * gated, block_ones[...]) * (1.0 / PD)
    low = gated * lax.rsqrt(mean + EPS) * params[1:2, :]
    low_out[:, :LANES] = att[...]
    low_out[:, LANES:] = low.astype(BF16)


def finish_back_kernel(
    docs,
    inner_width,
    meta,
    grad,
    y_in,
    act,
    cum,
    gate,
    params,
    spread,
    block_ones,
    gy_out,
    gate_out,
    params_out,
    state_out,
    so_far,
):
    c = pl.program_id(0)
    rows = act.shape[0]

    @pl.when(c == 0)
    def _():
        params_out[...] = jnp.zeros_like(params_out)
        state_out[...] = jnp.zeros_like(state_out)
        so_far[...] = jnp.zeros_like(so_far)

    row = c * rows + iota((rows, 1), 0)
    start = start_of(row, meta, docs)
    cum_now = cum[...]
    inner = act[:, :inner_width]
    skip, gain = (params[0:1, :], params[1:2, :])
    gate_now = gate[...]
    sig = sigmoid(gate_now)
    silu = gate_now * sig
    with_skip = y_in[...] + skip * inner
    gated = with_skip * silu
    ones = block_ones[...]
    scale = lax.rsqrt(split_nn(gated * gated, ones) * (1.0 / PD) + EPS)
    grad_now = grad[...]
    unit = gated * scale
    grad_unit = grad_now * gain
    mean = split_nn(grad_unit * unit, ones) * (1.0 / PD)
    grad_gated = scale * (grad_unit - unit * mean)
    grad_y = grad_gated * silu
    gy_out[...] = grad_y
    gate_out[...] = (grad_gated * with_skip * (sig * (1.0 + gate_now * (1.0 - sig)))).astype(BF16)
    params_out[0:1, :] += jnp.sum(grad_y * inner, axis=0, keepdims=True)
    params_out[1:2, :] += jnp.sum(grad_now * unit, axis=0, keepdims=True)
    inflow = jnp.where(start < 0, jnp.exp(cum_now + so_far[0:1, :]), 0.0)
    state_out[...] += low_tn(grad_y * split_nn(inflow, spread[...]), act[:, inner_width + NST :])
    so_far[...] = so_far[...] + jnp.broadcast_to(cum_now[rows - 1 : rows, :], so_far.shape)


def scan_back_kernel(
    docs,
    inner_width,
    meta,
    act,
    slope,
    step_in,
    sig_in,
    cum,
    grad_y_in,
    state_in,
    grad_end,
    mixed,
    edge,
    taps,
    heads,
    params,
    spread,
    spread_t,
    gmix_out,
    gstep_out,
    tail_out,
    edge_out,
    taps_out,
    heads_out,
    ext,
    grad_state,
):
    c = pl.num_programs(0) - 1 - pl.program_id(0)
    rows = act.shape[0]

    @pl.when(pl.program_id(0) == 0)
    def _():
        grad_state[...] = grad_end[...]
        ext[0:EDGE] = jnp.zeros((EDGE, ext.shape[1]), F32)
        ext[EDGE + rows :] = jnp.zeros((EDGE, ext.shape[1]), F32)
        taps_out[...] = jnp.zeros_like(taps_out)
        heads_out[...] = jnp.zeros_like(heads_out)

    @pl.when(pl.program_id(0) > 0)
    def _():
        ext[EDGE + rows :] = ext[EDGE : 2 * EDGE]

    at = c * rows
    row = at + iota((rows, 1), 0)
    start = start_of(row, meta, docs)
    last_start = start_of_one(at + rows - 1, meta, docs)
    inner = act[:, :inner_width]
    write = act[:, inner_width : inner_width + NST].astype(BF16)
    read = act[:, inner_width + NST :].astype(BF16)
    step = step_in[...]
    cum_now = cum[...]
    grad_y = grad_y_in[...]
    spread_now = spread[...]
    spread_back = spread_t[...]
    state = state_in[...]
    grads = grad_state[...]
    total = cum_now[rows - 1 : rows, :]
    step_wide = split_nn(step, spread_now)
    weighted = inner * step_wide
    tail = split_nn(jnp.where(row >= last_start, jnp.exp(total - cum_now), 0.0), spread_now)
    inflow = split_nn(jnp.where(start < at, jnp.exp(cum_now), 0.0), spread_now)
    kept_row = jnp.exp(total) * jnp.where(last_start < at, 1.0, 0.0)

    grads_low = grads.astype(BF16)
    state_low = state.astype(BF16)
    from_state = tail * product_nt(write, grads_low)
    leaving = split_nn(weighted * from_state, spread_back)
    grad_write = low_nn(tail * weighted, grads_low)
    arriving_y = inflow * grad_y
    arriving_low = arriving_y.astype(BF16)
    grad_read = product(arriving_low, state_low)
    arriving = split_nn(arriving_y * product_nt(read, state_low), spread_back)
    grad_state[...] = split_nt(
        spread_back, jnp.broadcast_to(kept_row, (NST, LANES))
    ) * grads + product_tn(arriving_low, read)
    both = split_nt(jnp.ones((8, NST), BF16), grads * state)
    kept_grad = kept_row * split_nn(both, spread_back)[0:1, :]
    grad_total = kept_grad + jnp.sum(leaving, axis=0, keepdims=True)

    couple_t = product_nt(write, read)
    at_key = iota((rows, rows), 0)
    at_query = iota((rows, rows), 1)
    end_row = at + iota((1, rows), 1)
    start_row = start_of(end_row, meta, docs) - at
    linked = (at_key >= start_row) & (at_key <= at_query)
    cum_t = cum_now.T
    lane = iota((rows, LANES), 1)
    sub = iota((LANES, rows), 0)
    weighted_low = weighted.astype(BF16)
    grad_y_low = grad_y.astype(BF16)
    grad_couple = jnp.zeros((rows, rows), F32)
    grad_cum = arriving - leaving
    grad_cum_t = jnp.zeros((LANES, rows), F32)
    pieces = []
    for pair in range(inner_width // LANES):
        span = slice(pair * LANES, (pair + 1) * LANES)
        values = weighted_low[:, span]
        grads_here = grad_y_low[:, span]
        results = []
        for side in range(2):
            head = 2 * pair + side
            arg = cum_t[head : head + 1, :] - cum_now[:, head : head + 1]
            decay = jnp.exp(jnp.where(linked, arg, MASKED))
            mine = jnp.where((lane >= PD) == (side == 1), values, jnp.zeros_like(values))
            grad_mixing = product_nt(mine, grads_here) * decay
            grad_couple = grad_couple + grad_mixing
            by_log = grad_mixing * couple_t
            grad_cum = grad_cum - jnp.where(
                lane == head, jnp.sum(by_log, axis=1, keepdims=True), 0.0
            )
            grad_cum_t = grad_cum_t + jnp.where(
                sub == head, jnp.sum(by_log, axis=0, keepdims=True), 0.0
            )
            results.append(product((couple_t * decay).astype(BF16), grads_here))
        pieces.append(jnp.where(lane < PD, results[0], results[1]))
    grad_weighted = jnp.concatenate(pieces, axis=1) + from_state
    grad_couple_low = grad_couple.astype(BF16)
    grad_write = grad_write + product(grad_couple_low, read)
    grad_read = grad_read + product_tn(grad_couple_low, write)

    grad_cum = grad_cum + grad_cum_t.T
    upper = (at_query >= at_key).astype(F32)
    grad_decay = (
        jnp.dot(upper, grad_cum, precision=HIGH, preferred_element_type=F32) + grad_total
    )
    rate = heads[1:2, :]
    grad_inner = grad_weighted * step_wide + grad_y * params[0:1, :]
    grad_step = split_nn(grad_weighted * inner, spread_back) - grad_decay * rate
    grad_raw = grad_step * sig_in[...]
    gstep_out[...] = grad_raw.astype(BF16)
    heads_out[0:1, :] += jnp.sum(grad_raw, axis=0, keepdims=True)
    heads_out[1:2, :] += jnp.sum(grad_decay * (-step * rate), axis=0, keepdims=True)

    grad_pre = jnp.concatenate([grad_inner, grad_write, grad_read], axis=1) * slope[...]
    ext[EDGE : EDGE + rows] = grad_pre
    taps_out[CONV : CONV + 1, :] += jnp.sum(grad_pre, axis=0, keepdims=True)
    mixed_now = mixed[...].astype(F32)
    grad_mixed = jnp.zeros_like(grad_pre)
    for lag in range(CONV):
        target = row + lag
        keep = (target - start_of(target, meta, docs) >= lag).astype(F32)
        moved = ext[EDGE + lag : EDGE + lag + rows] * keep
        grad_mixed = grad_mixed + taps[CONV - 1 - lag : CONV - lag, :] * moved
        taps_out[CONV - 1 - lag : CONV - lag, :] += jnp.sum(
            moved * mixed_now, axis=0, keepdims=True
        )
    gmix_out[...] = grad_mixed.astype(BF16)

    @pl.when(pl.program_id(0) == 0)
    def _():
        tail_out[...] = grad_mixed[rows - EDGE :]

    @pl.when(c == 0)
    def _():
        before = iota((EDGE, 1), 0) - EDGE
        edge_now = edge[...]
        grad_edge = jnp.zeros_like(edge_now)
        for lag in range(1, CONV):
            target = before + lag
            keep = (target - start_of(target, meta, docs) >= lag).astype(F32)
            moved = ext[lag : lag + EDGE] * keep
            grad_edge = grad_edge + taps[CONV - 1 - lag : CONV - lag, :] * moved
            taps_out[CONV - 1 - lag : CONV - lag, :] += jnp.sum(
                moved * edge_now, axis=0, keepdims=True
            )
        edge_out[...] = grad_edge


def call(kernel, grid, ins, outs, scratch=()):
    def spec(shape, block, index):
        if block == "smem":
            return pl.BlockSpec(memory_space=pltpu.SMEM)
        if block is None:
            return pl.BlockSpec(shape, lambda i: (0,) * len(shape))
        return pl.BlockSpec(block, index)

    return pl.pallas_call(
        kernel,
        grid=(grid,),
        in_specs=[spec(a.shape, block, index) for a, block, index in ins],
        out_specs=[spec(shape, block, index) for shape, _, block, index in outs],
        out_shape=[jax.ShapeDtypeStruct(shape, kind) for shape, kind, _, _ in outs],
        scratch_shapes=list(scratch),
        compiler_params=pltpu.CompilerParams(
            dimension_semantics=("arbitrary",), vmem_limit_bytes=VMEM_BYTES
        ),
    )(*[a for a, _, _ in ins])


def by_row(i):
    return (i, 0)


def exchange(values, axis, step):
    return lax.ppermute(values, axis, [(k, k ^ step) for k in range(lax.axis_size(axis))])


def bits_of(axis):
    return (lax.axis_size(axis) - 1).bit_length()


def bit_of(axis, bit):
    return (lax.axis_index(axis) >> bit) & 1


def scattered(values, axis, at, first_bit=0):
    for bit in range(first_bit, bits_of(axis)):
        shape = values.shape
        values = values.reshape(shape[:at] + (shape[at] // 2, 2) + shape[at + 1 :])
        mine = bit_of(axis, bit)
        kept = lax.dynamic_index_in_dim(values, mine, at + 1, False)
        sent = lax.dynamic_index_in_dim(values, 1 - mine, at + 1, False)
        values = (kept.astype(F32) + exchange(sent, axis, 1 << bit).astype(F32)).astype(BF16)
    return lax.squeeze(values, (at,))


def gathered(values, axis):
    bits = bits_of(axis)
    for place, bit in enumerate(reversed(range(bits))):
        other = exchange(values, axis, 1 << bit)
        upper = bit_of(axis, bit) == 1
        values = jnp.stack(
            [jnp.where(upper, other, values), jnp.where(upper, values, other)], axis=place
        )
    shape = values.shape[bits:]
    return values.reshape((lax.axis_size(axis),) + shape)


def summed_over(values, axes):
    for axis in axes:
        for bit in range(bits_of(axis)):
            values = values + exchange(values, axis, 1 << bit)
    return values


def to_owner(values, along):
    dp, ctx = (lax.axis_size(name) for name in WEIGHT_AXES)
    values = values.astype(BF16).reshape(dp, ctx, values.shape[0] // (dp * ctx), values.shape[1])
    if along == "ctx":
        return scattered(scattered(values, "ctx", 1), "dp", 0)
    return scattered(scattered(values, "dp", 0), "ctx", 0)


def chain(gathered, order, width, heads, reached):
    state = jnp.zeros((width, NST), F32)
    for k in order:
        own = gathered[k, :width].astype(F32)
        through = gathered[k, width].astype(F32) + gathered[k, width + 1].astype(F32)
        wide = jnp.repeat(through[:heads], PD)[:, None]
        state = jnp.where(reached(k), wide * state + own, state)
    return state


def rms_scale(values, gain):
    return values * lax.rsqrt(jnp.mean(values * values, axis=-1, keepdims=True) + EPS) * gain


def rms_back(values, gain, grad):
    scale = lax.rsqrt(jnp.mean(values * values, axis=-1, keepdims=True) + EPS)
    unit = values * scale
    inner = jnp.mean(grad * gain * values, axis=-1, keepdims=True)
    return (scale * (grad * gain - values * scale * scale * inner), jnp.sum(grad * unit, axis=0))


def body(
    tokens,
    cotangent,
    lengths,
    norm1_gain,
    norm2_gain,
    query_proj,
    keyval_proj,
    attn_proj,
    inner_proj,
    state_proj,
    step_proj,
    conv_inner,
    conv_state,
    step_bias,
    decay_log,
    skip_gain,
    mamba_gain,
    mamba_proj,
    gateup_proj,
    down_proj,
):
    rows = tokens.shape[0]
    rank = lax.axis_index("tp")
    ranks = lax.axis_size("tp")
    ctx_rank = lax.axis_index("ctx")
    ctx_size = lax.axis_size("ctx")
    pack = rows * ctx_size
    shard = query_proj.shape[0]
    width = inner_proj.shape[2]
    heads = width // PD
    mix = width + 2 * NST
    ff = gateup_proj.shape[2]
    docs = lengths.shape[1]
    quarter = rows // ranks
    chunks = rows // CHUNK
    kv_head = rank * (query_proj.shape[1] // HD) // (H // KVH)

    kv_shard = lax.dynamic_slice_in_dim(keyval_proj, kv_head * HD, HD, 2).reshape(shard, 2 * HD)
    step_shard = jnp.pad(step_proj, ((0, 0), (0, LANES - heads)))
    first_shard = jnp.concatenate(
        [
            inner_proj.reshape(shard, 2 * width),
            state_proj.reshape(shard, 2 * NST),
            query_proj,
            kv_shard,
            step_shard,
        ],
        axis=1,
    )
    mixer_shard = jnp.concatenate([attn_proj.T, mamba_proj.T], axis=1)
    early = lax.all_gather(
        jnp.concatenate([first_shard, mixer_shard], axis=1), WEIGHT_AXES, axis=0, tiled=True
    )
    first_w = early[:, : first_shard.shape[1]]
    mixer_w = early[:, first_shard.shape[1] :]
    late = lax.all_gather(
        jnp.concatenate([gateup_proj.reshape(shard, 2 * ff), down_proj.T], axis=1),
        WEIGHT_AXES,
        axis=0,
        tiled=True,
    )
    gateup_w = late[:, : 2 * ff]
    down_w = late[:, 2 * ff :]

    first_row = ctx_rank * rows
    bounds = jnp.cumsum(lengths[0])
    starts = bounds - lengths[0] - first_row
    meta = jnp.concatenate([starts, first_row[None]]).astype(jnp.int32)
    local = jnp.arange(rows, dtype=jnp.int32)
    doc_start = jnp.max(
        jnp.where(local[:, None] >= starts[None, :], starts[None, :], starts[0]), axis=1
    )
    frequency = ROPE_BASE ** (-jnp.arange(HD // 2, dtype=F32) / (HD // 2))
    angles = (local - doc_start).astype(F32)[:, None] * jnp.tile(frequency, 4)[None, :]
    sign = jnp.where(jnp.arange(LANES) % HD < HD // 2, -1.0, 1.0).astype(F32)
    cosine = jnp.cos(angles)
    sine = jnp.sin(angles) * sign[None, :]

    def mine(values, size, axis):
        return lax.dynamic_slice_in_dim(values, rank * size, size, axis)

    taps = jnp.concatenate([mine(conv_inner, width, 1), conv_state.reshape(CONV + 1, -1)], axis=1)
    taps = jnp.pad(taps, ((0, 8 - (CONV + 1)), (0, 0)))
    bias = mine(step_bias, heads, 0)
    rate = jnp.exp(mine(decay_log, heads, 0))
    head_params = jnp.pad(jnp.stack([bias, rate]), ((0, 6), (0, LANES - heads)))
    params = jnp.pad(
        jnp.stack([jnp.repeat(mine(skip_gain, heads, 0), PD), mine(mamba_gain, width, 0)]),
        ((0, 6), (0, 0)),
    )
    channel_head = jnp.arange(width) // PD
    spread = (jnp.arange(LANES)[:, None] == channel_head[None, :]).astype(BF16)
    spread_t = spread.T
    block_ones = (channel_head[:, None] == channel_head[None, :]).astype(BF16)

    hidden_in = tokens.astype(F32)
    normed = rms_scale(hidden_in, norm1_gain).astype(BF16)
    onward = [(source, source + 1) for source in range(ctx_size - 1)]
    backward = [(source + 1, source) for source in range(ctx_size - 1)]
    edge_tokens = lax.ppermute(tokens[rows - EDGE :], "ctx", onward).astype(F32)
    edge_normed = rms_scale(edge_tokens, norm1_gain).astype(BF16)
    proj = product(normed, first_w)
    edge = product(edge_normed, first_w[:, width : width + mix]).astype(BF16).astype(F32)

    chunk_128 = (CHUNK, LANES)
    chunk_mix = (CHUNK, mix)
    chunk_width = (CHUNK, width)
    q_rot, kv_local, mixed, act, slope, step, sig, cum, state_local, end = call(
        functools.partial(prep_kernel, docs, width),
        chunks,
        [
            (meta, "smem", None),
            (proj, (CHUNK, proj.shape[1]), by_row),
            (edge, None, None),
            (taps, None, None),
            (head_params, None, None),
            (cosine, chunk_128, by_row),
            (sine, chunk_128, by_row),
            (spread, None, None),
            (spread_t, None, None),
        ],
        [
            ((rows, LANES), BF16, chunk_128, by_row),
            ((rows, LANES), BF16, chunk_128, by_row),
            ((rows, mix), BF16, chunk_mix, by_row),
            ((rows, mix), F32, chunk_mix, by_row),
            ((rows, mix), F32, chunk_mix, by_row),
            ((rows, LANES), F32, chunk_128, by_row),
            ((rows, LANES), F32, chunk_128, by_row),
            ((rows, LANES), F32, chunk_128, by_row),
            ((chunks * width, NST), F32, (width, NST), by_row),
            ((width + 16, NST), BF16, None, None),
        ],
        [
            pltpu.VMEM((CHUNK + EDGE, mix), F32),
            pltpu.VMEM((width, NST), F32),
            pltpu.VMEM((8, LANES), F32),
        ],
    )
    ends = gathered(end, "ctx")
    kv_all = gathered(kv_local, "ctx").reshape(pack, LANES)
    (y_intra,) = call(
        functools.partial(intra_kernel, docs, width),
        chunks,
        [
            (meta, "smem", None),
            (act, chunk_mix, by_row),
            (step, chunk_128, by_row),
            (cum, chunk_128, by_row),
            (spread, None, None),
        ],
        [((rows, width), F32, chunk_width, by_row)],
    )
    blocks = rows // QUERY_BLOCK
    block_128 = (QUERY_BLOCK, LANES)
    attended, lse = call(
        functools.partial(attend_kernel, docs),
        blocks,
        [(meta, "smem", None), (q_rot, block_128, by_row), (kv_all, None, None)],
        [((rows, LANES), BF16, block_128, by_row), ((rows, LANES), F32, block_128, by_row)],
    )
    state_in = chain(ends, range(ctx_size - 1), width, heads, lambda k: k < ctx_rank)
    mixer_low, y, states = call(
        functools.partial(finish_kernel, docs, width),
        chunks,
        [
            (meta, "smem", None),
            (y_intra, chunk_width, by_row),
            (act, chunk_mix, by_row),
            (cum, chunk_128, by_row),
            (proj, chunk_width, by_row),
            (attended, chunk_128, by_row),
            (state_local, (width, NST), by_row),
            (state_in, None, None),
            (params, None, None),
            (spread, None, None),
            (spread_t, None, None),
            (block_ones, None, None),
        ],
        [
            ((rows, LANES + width), BF16, (CHUNK, LANES + width), by_row),
            ((rows, width), F32, chunk_width, by_row),
            ((chunks * width, NST), F32, (width, NST), by_row),
        ],
        [pltpu.VMEM((width, NST), F32)],
    )

    def scatter_rows(left, right):
        halves = left.reshape(ranks // 2, 2, quarter, left.shape[1])

        def half(which):
            chosen = lax.dynamic_index_in_dim(halves, which, 1, False)
            return product_nt(chosen.reshape(-1, left.shape[1]), right).astype(BF16)

        bit = bit_of("tp", 0)
        sent, kept = lax.optimization_barrier((half(1 - bit), half(bit)))
        values = kept.astype(F32) + exchange(sent, "tp", 1).astype(F32)
        values = values.astype(BF16).reshape(ranks // 2, quarter, right.shape[0])
        return scattered(values, "tp", 0, 1).astype(F32)

    def gather_rows(values):
        return gathered(values, "tp").reshape(rows, values.shape[1])

    hidden_q = mine(hidden_in, quarter, 0)
    residual = hidden_q + scatter_rows(mixer_low, mixer_w)
    normed2 = gather_rows(rms_scale(residual, norm2_gain).astype(BF16))
    gateup = product(normed2, gateup_w)
    gate, up = (gateup[:, :ff], gateup[:, ff:])
    gate_sig = jax.nn.sigmoid(gate)
    gate_silu = gate * gate_sig
    hidden_act = (gate_silu * up).astype(BF16)
    grad_hidden = product(cotangent, down_w)
    grad_gateup = jnp.concatenate(
        [grad_hidden * up * (gate_sig * (1.0 + gate * (1.0 - gate_sig))), grad_hidden * gate_silu],
        axis=1,
    ).astype(BF16)
    grad_norm2 = scatter_rows(grad_gateup, gateup_w)
    grad_values, norm2_part = rms_back(residual, norm2_gain, grad_norm2)
    grad_residual = mine(cotangent, quarter, 0).astype(F32) + grad_values
    late_terms = jnp.concatenate(
        [
            product_tn(normed2, grad_gateup).astype(BF16),
            product_tn(cotangent, hidden_act).astype(BF16),
        ],
        axis=1,
    )
    grad_residual, late_terms = lax.optimization_barrier((grad_residual, late_terms))
    late_grad = lax.psum_scatter(
        late_terms, WEIGHT_AXES, scatter_dimension=0, tiled=True
    ).astype(F32)
    gateup_grad = late_grad[:, : 2 * ff].reshape(gateup_proj.shape)
    down_grad = late_grad[:, 2 * ff :].T
    grad_mix = gather_rows(grad_residual.astype(BF16))
    layer_q = residual + scatter_rows(hidden_act, down_w)
    layer_out = gather_rows(layer_q.astype(BF16))

    grad_mixer = product(grad_mix, mixer_w)
    mixer_terms = product_tn(grad_mix, mixer_low)
    attn_grad = to_owner(mixer_terms[:, :LANES], "dp").astype(F32).T
    mamba_grad = to_owner(mixer_terms[:, LANES:], "ctx").astype(F32).T
    grad_att = grad_mixer[:, :LANES]
    grad_mamba = grad_mixer[:, LANES:]
    grad_y, grad_gate, params_grad, grad_in = call(
        functools.partial(finish_back_kernel, docs, width),
        chunks,
        [
            (meta, "smem", None),
            (grad_mamba, chunk_width, by_row),
            (y, chunk_width, by_row),
            (act, chunk_mix, by_row),
            (cum, chunk_128, by_row),
            (proj, chunk_width, by_row),
            (params, None, None),
            (spread, None, None),
            (block_ones, None, None),
        ],
        [
            ((rows, width), F32, chunk_width, by_row),
            ((rows, width), BF16, chunk_width, by_row),
            ((8, width), F32, None, None),
            ((width, NST), F32, None, None),
        ],
        [pltpu.VMEM((8, LANES), F32)],
    )
    grad_ins = gathered(jnp.concatenate([grad_in.astype(BF16), end[width:]], axis=0), "ctx")
    grad_query, grad_kv = call(
        functools.partial(attend_back_kernel, docs),
        blocks,
        [
            (meta, "smem", None),
            (q_rot, block_128, by_row),
            (kv_all, None, None),
            (grad_att, block_128, by_row),
            (attended, block_128, by_row),
            (lse, block_128, by_row),
            (cosine, block_128, by_row),
            (sine, block_128, by_row),
        ],
        [
            ((rows, LANES), BF16, block_128, by_row),
            ((pack, LANES), F32, None, None),
        ],
    )
    grad_kv = scattered(
        grad_kv.astype(BF16).reshape(ctx_size, rows, LANES), "ctx", 0
    ).astype(F32)
    half = HD // 2
    swapped = jnp.concatenate([grad_kv[:, half:HD], grad_kv[:, :half], grad_kv[:, HD:]], axis=1)
    is_key = jnp.arange(LANES)[None, :] < HD
    grad_kv = jnp.where(is_key, grad_kv * cosine - swapped * sine, grad_kv).astype(BF16)
    grad_end = chain(
        grad_ins, range(ctx_size - 1, 0, -1), width, heads, lambda k: k > ctx_rank
    )
    gate_terms = product_tn(normed, grad_gate).astype(BF16)
    gate_terms, grad_end = lax.optimization_barrier((gate_terms, grad_end))
    gate_owned = to_owner(gate_terms, "ctx").astype(F32)

    def back_row(i):
        return (chunks - 1 - i, 0)

    grad_mixed, grad_step, grad_tail, grad_edge, taps_grad, heads_grad = call(
        functools.partial(scan_back_kernel, docs, width),
        chunks,
        [
            (meta, "smem", None),
            (act, chunk_mix, back_row),
            (slope, chunk_mix, back_row),
            (step, chunk_128, back_row),
            (sig, chunk_128, back_row),
            (cum, chunk_128, back_row),
            (grad_y, chunk_width, back_row),
            (states, (width, NST), back_row),
            (grad_end, None, None),
            (mixed, chunk_mix, back_row),
            (edge, None, None),
            (taps, None, None),
            (head_params, None, None),
            (params, None, None),
            (spread, None, None),
            (spread_t, None, None),
        ],
        [
            ((rows, mix), BF16, chunk_mix, back_row),
            ((rows, LANES), BF16, chunk_128, back_row),
            ((EDGE, mix), F32, None, None),
            ((EDGE, mix), F32, None, None),
            ((8, mix), F32, None, None),
            ((8, LANES), F32, None, None),
        ],
        [pltpu.VMEM((CHUNK + 2 * EDGE, mix), F32), pltpu.VMEM((width, NST), F32)],
    )
    edge_grad = lax.ppermute(grad_edge, "ctx", backward)
    grad_mixed = lax.dynamic_update_slice_in_dim(
        grad_mixed, (grad_tail + edge_grad).astype(BF16), rows - EDGE, 0
    )
    grad_all = jnp.concatenate([grad_gate, grad_mixed, grad_query, grad_kv, grad_step], axis=1)
    base = width + mix
    split = base - NST
    owned_a = to_owner(product_tn(normed, grad_all[:, width:split]), "ctx").astype(F32)
    owned_b = to_owner(product_tn(normed, grad_all[:, split:]), "dp").astype(F32)
    grad_norm1 = scatter_rows(grad_all, first_w)
    grad_values, norm1_part = rms_back(hidden_q, norm1_gain, grad_norm1)
    tokens_grad = gather_rows((grad_residual + grad_values).astype(BF16))
    inner_grad = jnp.concatenate([gate_owned, owned_a[:, :width]], axis=1).reshape(
        inner_proj.shape
    )
    query_grad = owned_b[:, NST : NST + LANES]
    kv_owned = owned_b[:, NST + LANES : NST + 2 * LANES]
    step_grad = owned_b[:, NST + 2 * LANES : NST + 2 * LANES + heads]
    kv_wide = lax.dynamic_update_slice_in_dim(
        jnp.zeros(keyval_proj.shape, F32), kv_owned.reshape(shard, 2, HD), kv_head * HD, 2
    )
    shared = jnp.concatenate(
        [kv_wide.reshape(shard, -1), owned_a[:, width:], owned_b[:, :NST]], axis=1
    )
    shared = summed_over(shared, ("tp",))
    keyval_grad = shared[:, : 2 * KVH * HD].reshape(keyval_proj.shape)
    state_grad = shared[:, 2 * KVH * HD :].reshape(state_proj.shape)

    def flat(values):
        values = values.reshape(-1)
        return jnp.pad(values, (0, -values.shape[0] % LANES)).reshape(-1, LANES)

    def sum_small(parts, axes):
        sizes = [-(-part.size // LANES) for part in parts]
        total = summed_over(jnp.concatenate([flat(part) for part in parts], axis=0), axes)
        ends = [sum(sizes[: k + 1]) for k in range(len(parts))]
        return [total[end - size : end] for size, end in zip(sizes, ends)]

    own_parts = [
        taps_grad[: CONV + 1, :width],
        params_grad[1],
        heads_grad[0, :heads],
        heads_grad[1, :heads],
        jnp.sum(params_grad[0].reshape(heads, PD), axis=1),
    ]
    all_parts = [norm2_part, taps_grad[: CONV + 1, width:]]
    sums = sum_small(own_parts + all_parts, ("ctx", "dp"))
    norm2_grad, convst_grad = sum_small(sums[len(own_parts) :], ("tp",))
    wide = gathered(jnp.concatenate(sums[: len(own_parts)], axis=0), "tp")
    (norm1_grad,) = sum_small([norm1_part], ("tp", "ctx", "dp"))
    at = [0]
    for part in sums[: len(own_parts)]:
        at.append(at[-1] + part.shape[0])

    def of_heads(which, size):
        return wide[:, at[which] : at[which + 1]].reshape(ranks, -1)[:, :size]

    convin_grad = of_heads(0, (CONV + 1) * width).reshape(ranks, CONV + 1, width)
    convin_grad = convin_grad.transpose(1, 0, 2).reshape(conv_inner.shape)
    return (
        layer_out,
        tokens_grad,
        norm1_grad.reshape(norm1_gain.shape),
        norm2_grad.reshape(norm2_gain.shape),
        query_grad,
        keyval_grad,
        attn_grad,
        inner_grad,
        state_grad,
        step_grad,
        convin_grad,
        convst_grad.reshape(-1)[: conv_state.size].reshape(conv_state.shape),
        of_heads(2, heads).reshape(-1),
        of_heads(3, heads).reshape(-1),
        of_heads(4, heads).reshape(-1),
        of_heads(1, width).reshape(-1),
        mamba_grad,
        gateup_grad,
        down_grad,
    )


def solution(mesh):
    rows_split = P(("dp", "ctx"), None)
    split_0 = P(("dp", "ctx"), "tp")
    split_0_whole = P(("dp", "ctx"), None, None)
    split_0_last = P(("dp", "ctx"), None, "tp")
    split_1 = P("tp", ("dp", "ctx"))
    return jax.shard_map(
        body,
        mesh=mesh,
        in_specs=(
            rows_split,
            rows_split,
            P("dp", None),
            P(),
            P(),
            split_0,
            split_0_whole,
            split_1,
            split_0_last,
            split_0_whole,
            split_0,
            P(),
            P(),
            P(),
            P(),
            P(),
            P(),
            split_1,
            split_0_last,
            split_1,
        ),
        out_specs=(
            rows_split,
            rows_split,
            P(),
            P(),
            split_0,
            split_0_whole,
            split_1,
            split_0_last,
            split_0_whole,
            split_0,
            P(),
            P(),
            P(),
            P(),
            P(),
            P(),
            split_1,
            split_0_last,
            split_1,
        ),
        check_vma=False,
    )
```

```python
import functools

import jax
import jax.numpy as jnp
from jax import lax
from jax.experimental import pallas as pl
from jax.experimental.layout import Layout, with_layout_constraint
from jax.experimental.pallas import tpu as pltpu
from jax.sharding import PartitionSpec as P

H = 8
KVH = 2
HD = 64
PD = 64
NST = 128
CONV = 4
CHUNK = 256
QUERY_BLOCK = 256
KEY_BLOCK = 512
EDGE = 8
LANES = 128
VMEM_BYTES = 48 * 1024 * 1024

EPS = 1e-05
ROPE_BASE = 10000.0
MASKED = -1e30
HIGH = lax.Precision.HIGHEST
F32 = jnp.float32
BF16 = jnp.bfloat16
WEIGHT_AXES = ("dp", "ctx")


def product(left, right):
    return jnp.dot(left, right, preferred_element_type=F32)


def product_tn(left, right):
    return lax.dot_general(left, right, (((0,), (0,)), ((), ())), preferred_element_type=F32)


def product_nt(left, right):
    return lax.dot_general(left, right, (((1,), (1,)), ((), ())), preferred_element_type=F32)


def low_nn(left, right):
    return product(left.astype(BF16), right.astype(BF16))


def low_tn(left, right):
    return product_tn(left.astype(BF16), right.astype(BF16))


def low_nt(left, right):
    return product_nt(left.astype(BF16), right.astype(BF16))


def split_nn(left, ones):
    first = left.astype(BF16)
    second = (left - first.astype(F32)).astype(BF16)
    return product(first, ones) + product(second, ones)


def split_nt(ones, right):
    first = right.astype(BF16)
    second = (right - first.astype(F32)).astype(BF16)
    return product_nt(ones, first) + product_nt(ones, second)


def iota(shape, dim):
    return lax.broadcasted_iota(jnp.int32, shape, dim)


def start_of(rows, meta, docs):
    start = jnp.full(rows.shape, meta[0], jnp.int32)
    for doc in range(1, docs):
        start = jnp.where(rows >= meta[doc], meta[doc], start)
    return start


def start_of_one(row, meta, docs):
    start = meta[0]
    for doc in range(1, docs):
        start = jnp.where(row >= meta[doc], meta[doc], start)
    return start


def sigmoid(values):
    return 1.0 / (1.0 + jnp.exp(-values))


def swap_halves(values):
    lane = iota(values.shape, 1)
    up = pltpu.roll(values, LANES - HD // 2, 1)
    down = pltpu.roll(values, HD // 2, 1)
    return jnp.where(lane % HD < HD // 2, up, down)


def prep_kernel(
    docs,
    inner_width,
    meta,
    proj,
    edge,
    taps,
    heads,
    cosine,
    sine,
    spread,
    spread_t,
    q_out,
    kv_out,
    mixed_out,
    act_out,
    slope_out,
    step_out,
    sig_out,
    cum_out,
    state_out,
    end_out,
    ext,
    state,
    total_log,
):
    c = pl.program_id(0)
    rows = proj.shape[0]
    mix = ext.shape[1]
    row = c * rows + iota((rows, 1), 0)
    rel = row - start_of(row, meta, docs)
    mixed = proj[:, :mix].astype(BF16)
    mixed_out[...] = mixed

    @pl.when(c == 0)
    def _():
        ext[0:EDGE] = edge[...]
        state[...] = jnp.zeros_like(state)
        total_log[...] = jnp.zeros_like(total_log)

    @pl.when(c > 0)
    def _():
        ext[0:EDGE] = ext[rows : rows + EDGE]

    ext[EDGE : EDGE + rows] = mixed.astype(F32)
    pre = jnp.broadcast_to(taps[CONV : CONV + 1, :], (rows, mix))
    for lag in range(CONV):
        keep = (rel >= lag).astype(F32)
        pre = pre + taps[CONV - 1 - lag : CONV - lag, :] * (
            ext[EDGE - lag : EDGE - lag + rows] * keep
        )
    sig = sigmoid(pre)
    act = pre * sig
    act_out[...] = act
    slope_out[...] = sig * (1.0 + pre * (1.0 - sig))

    base = mix
    cos, sin = (cosine[...], sine[...])
    queries = proj[:, base : base + LANES]
    turned = queries * cos + swap_halves(queries) * sin
    q_out[...] = (turned * HD ** (-0.5)).astype(BF16)
    keyval = proj[:, base + LANES : base + 2 * LANES]
    is_key = iota(keyval.shape, 1) < HD
    kv_out[...] = jnp.where(is_key, keyval * cos + swap_halves(keyval) * sin, keyval).astype(BF16)

    raw = proj[:, base + 2 * LANES : base + 3 * LANES] + heads[0:1, :]
    step = jnp.maximum(raw, 0.0) + jnp.log1p(jnp.exp(-jnp.abs(raw)))
    decay = -step * heads[1:2, :]
    lower = (iota((rows, rows), 0) >= iota((rows, rows), 1)).astype(F32)
    cum = jnp.dot(lower, decay, precision=HIGH, preferred_element_type=F32)
    step_out[...] = step
    sig_out[...] = sigmoid(raw)
    cum_out[...] = cum

    last = c * rows + rows - 1
    last_start = start_of_one(last, meta, docs)
    total = cum[rows - 1 : rows, :]
    tail = jnp.where(row >= last_start, jnp.exp(total - cum), 0.0) * step
    goes_on = jnp.where(last_start < c * rows, 1.0, 0.0)
    kept = split_nt(spread_t[...], jnp.broadcast_to(jnp.exp(total) * goes_on, (NST, LANES)))
    state_out[...] = state[...]
    added = low_tn(act[:, :inner_width] * split_nn(tail, spread[...]), act[:, inner_width : inner_width + NST])
    state[...] = kept * state[...] + added
    total_log[...] = total_log[...] + jnp.broadcast_to(total, total_log.shape)

    @pl.when(c == pl.num_programs(0) - 1)
    def _():
        through = jnp.exp(total_log[0:1, :]) * jnp.where(last_start < 0, 1.0, 0.0)
        first = through.astype(BF16)
        second = (through - first.astype(F32)).astype(BF16)
        sub = iota((16, LANES), 0)
        end_out[0:inner_width] = state[...].astype(BF16)
        end_out[inner_width : inner_width + 16] = jnp.where(
            sub == 0, first.astype(F32), jnp.where(sub == 1, second.astype(F32), 0.0)
        ).astype(BF16)


def intra_kernel(docs, inner_width, meta, act, step, cum, spread, y_out):
    c = pl.program_id(0)
    rows = act.shape[0]
    row = iota((rows, 1), 0)
    first = start_of(c * rows + row, meta, docs) - c * rows
    col = iota((rows, rows), 1)
    linked = (col >= first) & (col <= iota((rows, rows), 0))
    couple = low_nt(act[:, inner_width + NST :], act[:, inner_width : inner_width + NST])
    weighted = (act[:, :inner_width] * split_nn(step[...], spread[...])).astype(BF16)
    cum_now = cum[...]
    cum_t = cum_now.T
    lane = iota((rows, LANES), 1)
    for pair in range(inner_width // LANES):
        values = weighted[:, pair * LANES : (pair + 1) * LANES]
        results = []
        for head in (2 * pair, 2 * pair + 1):
            arg = cum_now[:, head : head + 1] - cum_t[head : head + 1, :]
            mixing = couple * jnp.exp(jnp.where(linked, arg, MASKED))
            results.append(product(mixing.astype(BF16), values))
        y_out[:, pair * LANES : (pair + 1) * LANES] = jnp.where(lane < PD, results[0], results[1])


def two_heads(values, upper):
    values = values.astype(F32)
    lane = iota(values.shape, 1)
    rolled = pltpu.roll(values, HD, 1)
    keep = lane >= HD if upper else lane < HD
    pair = (rolled, values) if upper else (values, rolled)
    return jnp.concatenate([jnp.where(keep, part, 0.0) for part in pair], axis=0)


def attend_kernel(docs, meta, q, kv, out, lse_out):
    block = pl.program_id(0)
    rows = q.shape[0]
    first_row = meta[docs]
    row = block * rows + iota((rows, 1), 0)
    start = start_of(row, meta, docs)
    queries = two_heads(q[...], False).astype(BF16)
    low_block = (start_of_one(block * rows, meta, docs) + first_row) // KEY_BLOCK
    high_block = (first_row + (block + 1) * rows + KEY_BLOCK - 1) // KEY_BLOCK

    def one(index, sums):
        top, total, summed = sums
        at = pl.multiple_of(index * KEY_BLOCK, KEY_BLOCK)
        keyval = kv[pl.ds(at, KEY_BLOCK), :]
        scores = product_nt(queries, keyval)
        key = index * KEY_BLOCK - first_row + iota((rows, KEY_BLOCK), 1)
        allowed = (key >= start) & (key <= row)
        allowed = jnp.concatenate([allowed, allowed], axis=0)
        scores = jnp.where(allowed, scores, MASKED)
        new_top = jnp.maximum(top, jnp.max(scores, axis=1, keepdims=True))
        scale = jnp.exp(top - new_top)
        probs = jnp.exp(scores - new_top)
        total = total * scale + jnp.sum(probs, axis=1, keepdims=True)
        return (new_top, total, summed * scale + product(probs.astype(BF16), keyval))

    top, total, summed = lax.fori_loop(
        low_block,
        high_block,
        one,
        (
            jnp.full((2 * rows, 1), MASKED, F32),
            jnp.zeros((2 * rows, 1), F32),
            jnp.zeros((2 * rows, LANES), F32),
        ),
    )
    result = summed / total
    lse = top + jnp.log(total)
    lane = iota((rows, LANES), 1)
    out[...] = jnp.where(lane < HD, pltpu.roll(result[:rows], HD, 1), result[rows:]).astype(BF16)
    lse_out[...] = jnp.where(lane < HD, lse[:rows], lse[rows:])


def attend_back_kernel(docs, meta, q, kv, grad, att, lse, cosine, sine, gq_out, gkv_out):
    block = pl.program_id(0)
    rows = q.shape[0]
    first_row = meta[docs]

    @pl.when(block == 0)
    def _():
        gkv_out[...] = jnp.zeros_like(gkv_out)

    row = block * rows + iota((rows, 1), 0)
    start = start_of(row, meta, docs)
    queries = two_heads(q[...], False).astype(BF16)
    grads = two_heads(grad[...].astype(BF16), True)
    lse_now = lse[...]
    lse_col = jnp.concatenate([lse_now[:, 0:1], lse_now[:, HD : HD + 1]], axis=0)
    delta = jnp.sum(grads * two_heads(att[...], True), axis=1, keepdims=True)
    grads = grads.astype(BF16)
    low_block = (start_of_one(block * rows, meta, docs) + first_row) // KEY_BLOCK
    high_block = (first_row + (block + 1) * rows + KEY_BLOCK - 1) // KEY_BLOCK

    def one(index, summed):
        at = pl.multiple_of(index * KEY_BLOCK, KEY_BLOCK)
        keyval = kv[pl.ds(at, KEY_BLOCK), :]
        scores = product_nt(queries, keyval)
        key = index * KEY_BLOCK - first_row + iota((rows, KEY_BLOCK), 1)
        allowed = (key >= start) & (key <= row)
        allowed = jnp.concatenate([allowed, allowed], axis=0)
        probs = jnp.exp(jnp.where(allowed, scores - lse_col, MASKED))
        grad_scores = (probs * (product_nt(grads, keyval) - delta)).astype(BF16)
        gkv_out[pl.ds(at, KEY_BLOCK), :] += product_tn(grad_scores, queries) + product_tn(
            probs.astype(BF16), grads
        )
        return summed + product(grad_scores, keyval)

    summed = lax.fori_loop(low_block, high_block, one, jnp.zeros((2 * rows, LANES), F32))
    lane = iota((rows, LANES), 1)
    grad_q = jnp.where(lane < HD, summed[:rows], pltpu.roll(summed[rows:], HD, 1)) * HD ** (-0.5)
    gq_out[...] = (grad_q * cosine[...] - swap_halves(grad_q) * sine[...]).astype(BF16)


def finish_kernel(
    docs,
    inner_width,
    meta,
    y_in,
    act,
    cum,
    gate,
    att,
    state_local,
    state_in,
    params,
    spread,
    spread_t,
    block_ones,
    low_out,
    y_out,
    state_out,
    carry,
):
    c = pl.program_id(0)
    rows = act.shape[0]

    @pl.when(c == 0)
    def _():
        carry[...] = state_in[...]

    row = c * rows + iota((rows, 1), 0)
    start = start_of(row, meta, docs)
    last_start = start_of_one(c * rows + rows - 1, meta, docs)
    cum_now = cum[...]
    inflow = jnp.where(start < c * rows, jnp.exp(cum_now), 0.0)
    state = state_local[...] + carry[...]
    state_out[...] = state
    inner = act[:, :inner_width]
    y = y_in[...] + low_nt(act[:, inner_width + NST :], state) * split_nn(inflow, spread[...])
    y_out[...] = y
    total = jnp.exp(cum_now[rows - 1 : rows, :]) * jnp.where(last_start < c * rows, 1.0, 0.0)
    carry[...] = carry[...] * split_nt(spread_t[...], jnp.broadcast_to(total, (NST, LANES)))
    gate_now = gate[...]
    gated = (y + params[0:1, :] * inner) * (gate_now * sigmoid(gate_now))
    mean = split_nn(gated * gated, block_ones[...]) * (1.0 / PD)
    low = gated * lax.rsqrt(mean + EPS) * params[1:2, :]
    low_out[:, :LANES] = att[...]
    low_out[:, LANES:] = low.astype(BF16)


def finish_back_kernel(
    docs,
    inner_width,
    meta,
    grad,
    y_in,
    act,
    cum,
    gate,
    params,
    spread,
    block_ones,
    gy_out,
    gate_out,
    params_out,
    state_out,
    so_far,
):
    c = pl.program_id(0)
    rows = act.shape[0]

    @pl.when(c == 0)
    def _():
        params_out[...] = jnp.zeros_like(params_out)
        state_out[...] = jnp.zeros_like(state_out)
        so_far[...] = jnp.zeros_like(so_far)

    row = c * rows + iota((rows, 1), 0)
    start = start_of(row, meta, docs)
    cum_now = cum[...]
    inner = act[:, :inner_width]
    skip, gain = (params[0:1, :], params[1:2, :])
    gate_now = gate[...]
    sig = sigmoid(gate_now)
    silu = gate_now * sig
    with_skip = y_in[...] + skip * inner
    gated = with_skip * silu
    ones = block_ones[...]
    scale = lax.rsqrt(split_nn(gated * gated, ones) * (1.0 / PD) + EPS)
    grad_now = grad[...]
    unit = gated * scale
    grad_unit = grad_now * gain
    mean = split_nn(grad_unit * unit, ones) * (1.0 / PD)
    grad_gated = scale * (grad_unit - unit * mean)
    grad_y = grad_gated * silu
    gy_out[...] = grad_y
    gate_out[...] = (grad_gated * with_skip * (sig * (1.0 + gate_now * (1.0 - sig)))).astype(BF16)
    params_out[0:1, :] += jnp.sum(grad_y * inner, axis=0, keepdims=True)
    params_out[1:2, :] += jnp.sum(grad_now * unit, axis=0, keepdims=True)
    inflow = jnp.where(start < 0, jnp.exp(cum_now + so_far[0:1, :]), 0.0)
    state_out[...] += low_tn(grad_y * split_nn(inflow, spread[...]), act[:, inner_width + NST :])
    so_far[...] = so_far[...] + jnp.broadcast_to(cum_now[rows - 1 : rows, :], so_far.shape)


def scan_back_kernel(
    docs,
    inner_width,
    meta,
    act,
    slope,
    step_in,
    sig_in,
    cum,
    grad_y_in,
    state_in,
    grad_end,
    mixed,
    edge,
    taps,
    heads,
    params,
    spread,
    spread_t,
    gmix_out,
    gstep_out,
    tail_out,
    edge_out,
    taps_out,
    heads_out,
    ext,
    grad_state,
):
    c = pl.num_programs(0) - 1 - pl.program_id(0)
    rows = act.shape[0]

    @pl.when(pl.program_id(0) == 0)
    def _():
        grad_state[...] = grad_end[...]
        ext[0:EDGE] = jnp.zeros((EDGE, ext.shape[1]), F32)
        ext[EDGE + rows :] = jnp.zeros((EDGE, ext.shape[1]), F32)
        taps_out[...] = jnp.zeros_like(taps_out)
        heads_out[...] = jnp.zeros_like(heads_out)

    @pl.when(pl.program_id(0) > 0)
    def _():
        ext[EDGE + rows :] = ext[EDGE : 2 * EDGE]

    at = c * rows
    row = at + iota((rows, 1), 0)
    start = start_of(row, meta, docs)
    last_start = start_of_one(at + rows - 1, meta, docs)
    inner = act[:, :inner_width]
    write = act[:, inner_width : inner_width + NST].astype(BF16)
    read = act[:, inner_width + NST :].astype(BF16)
    step = step_in[...]
    cum_now = cum[...]
    grad_y = grad_y_in[...]
    spread_now = spread[...]
    spread_back = spread_t[...]
    state = state_in[...]
    grads = grad_state[...]
    total = cum_now[rows - 1 : rows, :]
    step_wide = split_nn(step, spread_now)
    weighted = inner * step_wide
    tail = split_nn(jnp.where(row >= last_start, jnp.exp(total - cum_now), 0.0), spread_now)
    inflow = split_nn(jnp.where(start < at, jnp.exp(cum_now), 0.0), spread_now)
    kept_row = jnp.exp(total) * jnp.where(last_start < at, 1.0, 0.0)

    grads_low = grads.astype(BF16)
    state_low = state.astype(BF16)
    from_state = tail * product_nt(write, grads_low)
    leaving = split_nn(weighted * from_state, spread_back)
    grad_write = low_nn(tail * weighted, grads_low)
    arriving_y = inflow * grad_y
    arriving_low = arriving_y.astype(BF16)
    grad_read = product(arriving_low, state_low)
    arriving = split_nn(arriving_y * product_nt(read, state_low), spread_back)
    grad_state[...] = split_nt(
        spread_back, jnp.broadcast_to(kept_row, (NST, LANES))
    ) * grads + product_tn(arriving_low, read)
    both = split_nt(jnp.ones((8, NST), BF16), grads * state)
    kept_grad = kept_row * split_nn(both, spread_back)[0:1, :]
    grad_total = kept_grad + jnp.sum(leaving, axis=0, keepdims=True)

    couple_t = product_nt(write, read)
    at_key = iota((rows, rows), 0)
    at_query = iota((rows, rows), 1)
    end_row = at + iota((1, rows), 1)
    start_row = start_of(end_row, meta, docs) - at
    linked = (at_key >= start_row) & (at_key <= at_query)
    cum_t = cum_now.T
    lane = iota((rows, LANES), 1)
    sub = iota((LANES, rows), 0)
    weighted_low = weighted.astype(BF16)
    grad_y_low = grad_y.astype(BF16)
    grad_couple = jnp.zeros((rows, rows), F32)
    grad_cum = arriving - leaving
    grad_cum_t = jnp.zeros((LANES, rows), F32)
    pieces = []
    for pair in range(inner_width // LANES):
        span = slice(pair * LANES, (pair + 1) * LANES)
        values = weighted_low[:, span]
        grads_here = grad_y_low[:, span]
        results = []
        for side in range(2):
            head = 2 * pair + side
            arg = cum_t[head : head + 1, :] - cum_now[:, head : head + 1]
            decay = jnp.exp(jnp.where(linked, arg, MASKED))
            mine = jnp.where((lane >= PD) == (side == 1), values, jnp.zeros_like(values))
            grad_mixing = product_nt(mine, grads_here) * decay
            grad_couple = grad_couple + grad_mixing
            by_log = grad_mixing * couple_t
            grad_cum = grad_cum - jnp.where(
                lane == head, jnp.sum(by_log, axis=1, keepdims=True), 0.0
            )
            grad_cum_t = grad_cum_t + jnp.where(
                sub == head, jnp.sum(by_log, axis=0, keepdims=True), 0.0
            )
            results.append(product((couple_t * decay).astype(BF16), grads_here))
        pieces.append(jnp.where(lane < PD, results[0], results[1]))
    grad_weighted = jnp.concatenate(pieces, axis=1) + from_state
    grad_couple_low = grad_couple.astype(BF16)
    grad_write = grad_write + product(grad_couple_low, read)
    grad_read = grad_read + product_tn(grad_couple_low, write)

    grad_cum = grad_cum + grad_cum_t.T
    upper = (at_query >= at_key).astype(F32)
    grad_decay = (
        jnp.dot(upper, grad_cum, precision=HIGH, preferred_element_type=F32) + grad_total
    )
    rate = heads[1:2, :]
    grad_inner = grad_weighted * step_wide + grad_y * params[0:1, :]
    grad_step = split_nn(grad_weighted * inner, spread_back) - grad_decay * rate
    grad_raw = grad_step * sig_in[...]
    gstep_out[...] = grad_raw.astype(BF16)
    heads_out[0:1, :] += jnp.sum(grad_raw, axis=0, keepdims=True)
    heads_out[1:2, :] += jnp.sum(grad_decay * (-step * rate), axis=0, keepdims=True)

    grad_pre = jnp.concatenate([grad_inner, grad_write, grad_read], axis=1) * slope[...]
    ext[EDGE : EDGE + rows] = grad_pre
    taps_out[CONV : CONV + 1, :] += jnp.sum(grad_pre, axis=0, keepdims=True)
    mixed_now = mixed[...].astype(F32)
    grad_mixed = jnp.zeros_like(grad_pre)
    for lag in range(CONV):
        target = row + lag
        keep = (target - start_of(target, meta, docs) >= lag).astype(F32)
        moved = ext[EDGE + lag : EDGE + lag + rows] * keep
        grad_mixed = grad_mixed + taps[CONV - 1 - lag : CONV - lag, :] * moved
        taps_out[CONV - 1 - lag : CONV - lag, :] += jnp.sum(
            moved * mixed_now, axis=0, keepdims=True
        )
    gmix_out[...] = grad_mixed.astype(BF16)

    @pl.when(pl.program_id(0) == 0)
    def _():
        tail_out[...] = grad_mixed[rows - EDGE :]

    @pl.when(c == 0)
    def _():
        before = iota((EDGE, 1), 0) - EDGE
        edge_now = edge[...]
        grad_edge = jnp.zeros_like(edge_now)
        for lag in range(1, CONV):
            target = before + lag
            keep = (target - start_of(target, meta, docs) >= lag).astype(F32)
            moved = ext[lag : lag + EDGE] * keep
            grad_edge = grad_edge + taps[CONV - 1 - lag : CONV - lag, :] * moved
            taps_out[CONV - 1 - lag : CONV - lag, :] += jnp.sum(
                moved * edge_now, axis=0, keepdims=True
            )
        edge_out[...] = grad_edge


def feed_kernel(ff, normed, cotangent, weights, act_out, grad_out, back_out, forward_out):
    gateup_w = weights[:, : 2 * ff]
    down_w = weights[:, 2 * ff :]
    grad_hidden = product(cotangent[...], down_w)
    gateup = product(normed[...], gateup_w)
    gate, up = (gateup[:, :ff], gateup[:, ff:])
    sig = sigmoid(gate)
    silu = gate * sig
    act = (silu * up).astype(BF16)
    act_out[...] = act
    grad_gate = grad_hidden * up * (sig * (1.0 + gate * (1.0 - sig)))
    grad = jnp.concatenate([grad_gate, grad_hidden * silu], axis=1).astype(BF16)
    grad_out[...] = grad
    back_out[...] = product_nt(grad, gateup_w).astype(BF16)
    forward_out[...] = product_nt(act, down_w).astype(BF16)


def call(kernel, grid, ins, outs, scratch=()):
    def spec(shape, block, index):
        if block == "smem":
            return pl.BlockSpec(memory_space=pltpu.SMEM)
        if block is None:
            return pl.BlockSpec(shape, lambda i: (0,) * len(shape))
        return pl.BlockSpec(block, index)

    return pl.pallas_call(
        kernel,
        grid=(grid,),
        in_specs=[spec(a.shape, block, index) for a, block, index in ins],
        out_specs=[spec(shape, block, index) for shape, _, block, index in outs],
        out_shape=[jax.ShapeDtypeStruct(shape, kind) for shape, kind, _, _ in outs],
        scratch_shapes=list(scratch),
        compiler_params=pltpu.CompilerParams(
            dimension_semantics=("arbitrary",), vmem_limit_bytes=VMEM_BYTES
        ),
    )(*[a for a, _, _ in ins])


def by_row(i):
    return (i, 0)


def exchange(values, axis, step):
    return lax.ppermute(values, axis, [(k, k ^ step) for k in range(lax.axis_size(axis))])


def bits_of(axis):
    return (lax.axis_size(axis) - 1).bit_length()


def bit_of(axis, bit):
    return (lax.axis_index(axis) >> bit) & 1


def halved(values, axis, at, bit):
    shape = values.shape
    values = values.reshape(shape[:at] + (shape[at] // 2, 2) + shape[at + 1 :])
    mine = bit_of(axis, bit)
    kept = lax.dynamic_index_in_dim(values, mine, at + 1, False)
    sent = lax.dynamic_index_in_dim(values, 1 - mine, at + 1, False)
    return (kept.astype(F32) + exchange(sent, axis, 1 << bit).astype(F32)).astype(BF16)


def scattered(values, axis, at, first_bit=0):
    for bit in range(first_bit, bits_of(axis)):
        values = halved(values, axis, at, bit)
    return lax.squeeze(values, (at,))


def gathered(values, axis):
    bits = bits_of(axis)
    for place, bit in enumerate(reversed(range(bits))):
        other = exchange(values, axis, 1 << bit)
        upper = bit_of(axis, bit) == 1
        values = jnp.stack(
            [jnp.where(upper, other, values), jnp.where(upper, values, other)], axis=place
        )
    shape = values.shape[bits:]
    return values.reshape((lax.axis_size(axis),) + shape)


def summed_over(values, axes):
    for axis in axes:
        for bit in range(bits_of(axis)):
            values = values + exchange(values, axis, 1 << bit)
    return values


class Owned:
    def __init__(self, terms, along):
        dp, ctx = (lax.axis_size(name) for name in WEIGHT_AXES)
        rows, columns = terms.shape
        self.shape = (rows // (dp * ctx), columns)
        self.values = terms.astype(BF16).reshape((dp, ctx) + self.shape)
        over_ctx = [("ctx", 1, bit) for bit in range(bits_of("ctx"))]
        over_dp = [("dp", 0, bit) for bit in range(bits_of("dp"))]
        self.steps = over_ctx + over_dp if along == "ctx" else over_dp + over_ctx

    def step(self):
        if self.steps:
            self.values = halved(self.values, *self.steps.pop(0))

    def result(self):
        while self.steps:
            self.step()
        return self.values.reshape(self.shape).astype(F32)


def in_order(owned, *others):
    values, others = lax.optimization_barrier(([one.values for one in owned], others))
    for one, value in zip(owned, values):
        one.values = value
    return others


def chain(gathered, order, width, heads, reached):
    state = jnp.zeros((width, NST), F32)
    for k in order:
        own = gathered[k, :width].astype(F32)
        through = gathered[k, width].astype(F32) + gathered[k, width + 1].astype(F32)
        wide = jnp.repeat(through[:heads], PD)[:, None]
        state = jnp.where(reached(k), wide * state + own, state)
    return state


def rms_scale(values, gain):
    return values * lax.rsqrt(jnp.mean(values * values, axis=-1, keepdims=True) + EPS) * gain


def rms_back(values, gain, grad):
    scale = lax.rsqrt(jnp.mean(values * values, axis=-1, keepdims=True) + EPS)
    unit = values * scale
    inner = jnp.mean(grad * gain * values, axis=-1, keepdims=True)
    return (scale * (grad * gain - values * scale * scale * inner), jnp.sum(grad * unit, axis=0))


def body(
    tokens,
    cotangent,
    lengths,
    norm1_gain,
    norm2_gain,
    query_proj,
    keyval_proj,
    attn_proj,
    inner_proj,
    state_proj,
    step_proj,
    conv_inner,
    conv_state,
    step_bias,
    decay_log,
    skip_gain,
    mamba_gain,
    mamba_proj,
    gateup_proj,
    down_proj,
):
    rows = tokens.shape[0]
    rank = lax.axis_index("tp")
    ranks = lax.axis_size("tp")
    ctx_rank = lax.axis_index("ctx")
    ctx_size = lax.axis_size("ctx")
    pack = rows * ctx_size
    shard = query_proj.shape[0]
    width = inner_proj.shape[2]
    heads = width // PD
    mix = width + 2 * NST
    ff = gateup_proj.shape[2]
    docs = lengths.shape[1]
    quarter = rows // ranks
    chunks = rows // CHUNK
    kv_head = rank * (query_proj.shape[1] // HD) // (H // KVH)

    kv_shard = lax.dynamic_slice_in_dim(keyval_proj, kv_head * HD, HD, 2).reshape(shard, 2 * HD)
    step_shard = jnp.pad(step_proj, ((0, 0), (0, LANES - heads)))
    inner_shard = inner_proj.reshape(shard, 2 * width)
    first_shard = jnp.concatenate(
        [inner_shard[:, width:], state_proj.reshape(shard, 2 * NST), query_proj, kv_shard, step_shard],
        axis=1,
    )
    mixer_shard = jnp.concatenate([inner_shard[:, :width], attn_proj.T, mamba_proj.T], axis=1)
    last_shard = jnp.concatenate([gateup_proj.reshape(shard, 2 * ff), down_proj.T], axis=1)

    def whole(part):
        return lax.all_gather(part, WEIGHT_AXES, axis=0, tiled=True)

    first_w = whole(first_shard)
    second_w = whole(mixer_shard)
    gate_w = second_w[:, :width]
    mixer_w = second_w[:, width:]
    last_w = whole(last_shard)

    first_row = ctx_rank * rows
    bounds = jnp.cumsum(lengths[0])
    starts = bounds - lengths[0] - first_row
    meta = jnp.concatenate([starts, first_row[None]]).astype(jnp.int32)
    local = jnp.arange(rows, dtype=jnp.int32)
    doc_start = jnp.max(
        jnp.where(local[:, None] >= starts[None, :], starts[None, :], starts[0]), axis=1
    )
    frequency = ROPE_BASE ** (-jnp.arange(HD // 2, dtype=F32) / (HD // 2))
    angles = (local - doc_start).astype(F32)[:, None] * jnp.tile(frequency, 4)[None, :]
    sign = jnp.where(jnp.arange(LANES) % HD < HD // 2, -1.0, 1.0).astype(F32)
    cosine = jnp.cos(angles)
    sine = jnp.sin(angles) * sign[None, :]

    def mine(values, size, axis):
        return lax.dynamic_slice_in_dim(values, rank * size, size, axis)

    taps = jnp.concatenate([mine(conv_inner, width, 1), conv_state.reshape(CONV + 1, -1)], axis=1)
    taps = jnp.pad(taps, ((0, 8 - (CONV + 1)), (0, 0)))
    bias = mine(step_bias, heads, 0)
    rate = jnp.exp(mine(decay_log, heads, 0))
    head_params = jnp.pad(jnp.stack([bias, rate]), ((0, 6), (0, LANES - heads)))
    params = jnp.pad(
        jnp.stack([jnp.repeat(mine(skip_gain, heads, 0), PD), mine(mamba_gain, width, 0)]),
        ((0, 6), (0, 0)),
    )
    channel_head = jnp.arange(width) // PD
    spread = (jnp.arange(LANES)[:, None] == channel_head[None, :]).astype(BF16)
    spread_t = spread.T
    block_ones = (channel_head[:, None] == channel_head[None, :]).astype(BF16)

    normed = lax.optimization_barrier(rms_scale(tokens.astype(F32), norm1_gain).astype(BF16))
    onward = [(source, source + 1) for source in range(ctx_size - 1)]
    backward = [(source + 1, source) for source in range(ctx_size - 1)]
    edge_tokens = lax.ppermute(tokens[rows - EDGE :], "ctx", onward).astype(F32)
    edge_normed = rms_scale(edge_tokens, norm1_gain).astype(BF16)
    proj = product(normed, first_w)
    edge = product(edge_normed, first_w[:, :mix]).astype(BF16).astype(F32)

    chunk_128 = (CHUNK, LANES)
    chunk_mix = (CHUNK, mix)
    chunk_width = (CHUNK, width)
    q_rot, kv_local, mixed, act, slope, step, sig, cum, state_local, end = call(
        functools.partial(prep_kernel, docs, width),
        chunks,
        [
            (meta, "smem", None),
            (proj, (CHUNK, proj.shape[1]), by_row),
            (edge, None, None),
            (taps, None, None),
            (head_params, None, None),
            (cosine, chunk_128, by_row),
            (sine, chunk_128, by_row),
            (spread, None, None),
            (spread_t, None, None),
        ],
        [
            ((rows, LANES), BF16, chunk_128, by_row),
            ((rows, LANES), BF16, chunk_128, by_row),
            ((rows, mix), BF16, chunk_mix, by_row),
            ((rows, mix), F32, chunk_mix, by_row),
            ((rows, mix), F32, chunk_mix, by_row),
            ((rows, LANES), F32, chunk_128, by_row),
            ((rows, LANES), F32, chunk_128, by_row),
            ((rows, LANES), F32, chunk_128, by_row),
            ((chunks * width, NST), F32, (width, NST), by_row),
            ((width + 16, NST), BF16, None, None),
        ],
        [
            pltpu.VMEM((CHUNK + EDGE, mix), F32),
            pltpu.VMEM((width, NST), F32),
            pltpu.VMEM((8, LANES), F32),
        ],
    )
    ends = gathered(end, "ctx")
    kv_all = gathered(kv_local, "ctx").reshape(pack, LANES)
    (y_intra,) = call(
        functools.partial(intra_kernel, docs, width),
        chunks,
        [
            (meta, "smem", None),
            (act, chunk_mix, by_row),
            (step, chunk_128, by_row),
            (cum, chunk_128, by_row),
            (spread, None, None),
        ],
        [((rows, width), F32, chunk_width, by_row)],
    )
    blocks = rows // QUERY_BLOCK
    block_128 = (QUERY_BLOCK, LANES)
    attended, lse = call(
        functools.partial(attend_kernel, docs),
        blocks,
        [(meta, "smem", None), (q_rot, block_128, by_row), (kv_all, None, None)],
        [((rows, LANES), BF16, block_128, by_row), ((rows, LANES), F32, block_128, by_row)],
    )
    normed_again, _ = lax.optimization_barrier((normed, (attended, y_intra)))
    gate_z = product(normed_again, gate_w)
    state_in = chain(ends, range(ctx_size - 1), width, heads, lambda k: k < ctx_rank)
    mixer_low, y, states = call(
        functools.partial(finish_kernel, docs, width),
        chunks,
        [
            (meta, "smem", None),
            (y_intra, chunk_width, by_row),
            (act, chunk_mix, by_row),
            (cum, chunk_128, by_row),
            (gate_z, chunk_width, by_row),
            (attended, chunk_128, by_row),
            (state_local, (width, NST), by_row),
            (state_in, None, None),
            (params, None, None),
            (spread, None, None),
            (spread_t, None, None),
            (block_ones, None, None),
        ],
        [
            ((rows, LANES + width), BF16, (CHUNK, LANES + width), by_row),
            ((rows, width), F32, chunk_width, by_row),
            ((chunks * width, NST), F32, (width, NST), by_row),
        ],
        [pltpu.VMEM((width, NST), F32)],
    )

    def scatter_rows(values, first_after=(), then_after=()):
        values, _ = lax.optimization_barrier((values, first_after))
        values = values.reshape(ranks, quarter, values.shape[1])
        values = halved(values, "tp", 0, 0)
        values, _ = lax.optimization_barrier((values, then_after))
        return scattered(values, "tp", 0, 1).astype(F32)

    def scatter_product(left, right):
        halves = left.reshape(ranks // 2, 2, quarter, left.shape[1])

        def half(which):
            chosen = lax.dynamic_index_in_dim(halves, which, 1, False)
            return product_nt(chosen.reshape(-1, left.shape[1]), right).astype(BF16)

        bit = bit_of("tp", 0)
        sent, kept = lax.optimization_barrier((half(1 - bit), half(bit)))
        values = kept.astype(F32) + exchange(sent, "tp", 1).astype(F32)
        values = values.astype(BF16).reshape(ranks // 2, quarter, right.shape[0])
        return scattered(values, "tp", 0, 1).astype(F32)

    def row_major(values):
        return with_layout_constraint(values, Layout(major_to_minor=(0, 1)))

    def gather_rows(values):
        return gathered(values, "tp").reshape(rows, values.shape[1])

    hidden_q = mine(tokens, quarter, 0).astype(F32)
    residual = hidden_q + scatter_product(mixer_low, mixer_w)
    normed2 = gather_rows(rms_scale(residual, norm2_gain).astype(BF16))
    row_block = (CHUNK, tokens.shape[1])
    hidden_act, grad_gateup, back_part, forward_part = call(
        functools.partial(feed_kernel, ff),
        chunks,
        [
            (normed2, row_block, by_row),
            (cotangent, row_block, by_row),
            (last_w, None, None),
        ],
        [
            ((rows, ff), BF16, (CHUNK, ff), by_row),
            ((rows, 2 * ff), BF16, (CHUNK, 2 * ff), by_row),
            (tokens.shape, BF16, row_block, by_row),
            (tokens.shape, BF16, row_block, by_row),
        ],
    )
    grad_norm2 = scatter_rows(back_part)
    grad_values, norm2_part = rms_back(residual, norm2_gain, grad_norm2)
    grad_residual = mine(cotangent, quarter, 0).astype(F32) + grad_values
    late_terms = row_major(
        jnp.concatenate(
            [
                product_tn(normed2, grad_gateup).astype(BF16),
                product_tn(cotangent, hidden_act).astype(BF16),
            ],
            axis=1,
        )
    )
    grad_residual, late_terms = lax.optimization_barrier((grad_residual, late_terms))
    late_grad = lax.psum_scatter(
        late_terms, WEIGHT_AXES, scatter_dimension=0, tiled=True
    ).astype(F32)
    gateup_grad = late_grad[:, : 2 * ff].reshape(gateup_proj.shape)
    down_grad = late_grad[:, 2 * ff :].T
    grad_mix = gather_rows(grad_residual.astype(BF16))
    layer_half = scatter_rows(forward_part, grad_residual, grad_mix)
    layer_q = (residual + layer_half).astype(BF16)

    grad_mixer = product(grad_mix, mixer_w)
    mixer_terms = product_tn(grad_mix, mixer_low).astype(BF16)
    grad_att = grad_mixer[:, :LANES]
    grad_mamba = grad_mixer[:, LANES:]
    grad_y, grad_gate, params_grad, grad_in = call(
        functools.partial(finish_back_kernel, docs, width),
        chunks,
        [
            (meta, "smem", None),
            (grad_mamba, chunk_width, by_row),
            (y, chunk_width, by_row),
            (act, chunk_mix, by_row),
            (cum, chunk_128, by_row),
            (gate_z, chunk_width, by_row),
            (params, None, None),
            (spread, None, None),
            (block_ones, None, None),
        ],
        [
            ((rows, width), F32, chunk_width, by_row),
            ((rows, width), BF16, chunk_width, by_row),
            ((8, width), F32, None, None),
            ((width, NST), F32, None, None),
        ],
        [pltpu.VMEM((8, LANES), F32)],
    )
    grad_ins = gathered(jnp.concatenate([grad_in.astype(BF16), end[width:]], axis=0), "ctx")
    grad_query, grad_kv = call(
        functools.partial(attend_back_kernel, docs),
        blocks,
        [
            (meta, "smem", None),
            (q_rot, block_128, by_row),
            (kv_all, None, None),
            (grad_att, block_128, by_row),
            (attended, block_128, by_row),
            (lse, block_128, by_row),
            (cosine, block_128, by_row),
            (sine, block_128, by_row),
        ],
        [
            ((rows, LANES), BF16, block_128, by_row),
            ((pack, LANES), F32, None, None),
        ],
    )
    grad_kv = scattered(
        grad_kv.astype(BF16).reshape(ctx_size, rows, LANES), "ctx", 0
    ).astype(F32)
    half = HD // 2
    swapped = jnp.concatenate([grad_kv[:, half:HD], grad_kv[:, :half], grad_kv[:, HD:]], axis=1)
    is_key = jnp.arange(LANES)[None, :] < HD
    grad_kv = jnp.where(is_key, grad_kv * cosine - swapped * sine, grad_kv).astype(BF16)
    grad_end = chain(
        grad_ins, range(ctx_size - 1, 0, -1), width, heads, lambda k: k > ctx_rank
    )
    gate_terms = product_tn(normed, jnp.concatenate([grad_gate, grad_query], axis=1)).astype(BF16)
    second_terms = row_major(jnp.concatenate([mixer_terms, gate_terms], axis=1))
    second_terms, grad_end, layer_q = lax.optimization_barrier((second_terms, grad_end, layer_q))
    second_grad = lax.psum_scatter(
        second_terms, WEIGHT_AXES, scatter_dimension=0, tiled=True
    ).astype(F32)
    attn_grad = second_grad[:, :LANES].T
    mamba_grad = second_grad[:, LANES : LANES + width].T
    query_grad = second_grad[:, LANES + 2 * width :]
    layer_out = gather_rows(layer_q)

    def back_row(i):
        return (chunks - 1 - i, 0)

    grad_mixed, grad_step, grad_tail, grad_edge, taps_grad, heads_grad = call(
        functools.partial(scan_back_kernel, docs, width),
        chunks,
        [
            (meta, "smem", None),
            (act, chunk_mix, back_row),
            (slope, chunk_mix, back_row),
            (step, chunk_128, back_row),
            (sig, chunk_128, back_row),
            (cum, chunk_128, back_row),
            (grad_y, chunk_width, back_row),
            (states, (width, NST), back_row),
            (grad_end, None, None),
            (mixed, chunk_mix, back_row),
            (edge, None, None),
            (taps, None, None),
            (head_params, None, None),
            (params, None, None),
            (spread, None, None),
            (spread_t, None, None),
        ],
        [
            ((rows, mix), BF16, chunk_mix, back_row),
            ((rows, LANES), BF16, chunk_128, back_row),
            ((EDGE, mix), F32, None, None),
            ((EDGE, mix), F32, None, None),
            ((8, mix), F32, None, None),
            ((8, LANES), F32, None, None),
        ],
        [pltpu.VMEM((CHUNK + 2 * EDGE, mix), F32), pltpu.VMEM((width, NST), F32)],
    )
    edge_grad = lax.ppermute(grad_edge, "ctx", backward)
    grad_mixed = lax.dynamic_update_slice_in_dim(
        grad_mixed, (grad_tail + edge_grad).astype(BF16), rows - EDGE, 0
    )
    mixed_a = grad_mixed[:, : width + NST]
    mixed_b = jnp.concatenate([grad_mixed[:, width + NST :], grad_kv, grad_step], axis=1)
    late_a = Owned(product_tn(normed, mixed_a), "ctx")
    late_b = Owned(product_tn(normed, mixed_b), "dp")
    grad_all = jnp.concatenate([grad_mixed, grad_query, grad_kv, grad_step, grad_gate], axis=1)
    all_w = jnp.concatenate([first_w, gate_w], axis=1)
    (grad_all,) = in_order([late_a, late_b], grad_all)
    late_a.step()
    late_b.step()
    grad_norm1 = scatter_product(grad_all, all_w)
    grad_values, norm1_part = rms_back(hidden_q, norm1_gain, grad_norm1)
    tokens_grad = gather_rows((grad_residual + grad_values).astype(BF16))
    owned_a = late_a.result()
    owned_b = late_b.result()
    inner_grad = jnp.concatenate(
        [second_grad[:, LANES + width : LANES + 2 * width], owned_a[:, :width]], axis=1
    ).reshape(inner_proj.shape)
    kv_owned = owned_b[:, NST : NST + LANES]
    step_grad = owned_b[:, NST + LANES : NST + LANES + heads]
    kv_wide = lax.dynamic_update_slice_in_dim(
        jnp.zeros(keyval_proj.shape, F32), kv_owned.reshape(shard, 2, HD), kv_head * HD, 2
    )
    shared = jnp.concatenate(
        [kv_wide.reshape(shard, -1), owned_a[:, width:], owned_b[:, :NST]], axis=1
    ).astype(BF16)
    for bit in range(bits_of("tp")):
        other = exchange(shared, "tp", 1 << bit).astype(F32)
        shared = shared.astype(F32) + other
        if bit + 1 < bits_of("tp"):
            shared = shared.astype(BF16)
    keyval_grad = shared[:, : 2 * KVH * HD].reshape(keyval_proj.shape)
    state_grad = shared[:, 2 * KVH * HD :].reshape(state_proj.shape)

    norms = jnp.concatenate([norm1_part.reshape(8, -1), norm2_part.reshape(8, -1)], axis=1)
    small = jnp.concatenate([taps_grad, heads_grad, params_grad, norms], axis=1)
    small = gathered(summed_over(small, ("ctx", "dp")), "tp")
    at = mix + LANES
    convin_grad = small[:, : CONV + 1, :width].transpose(1, 0, 2).reshape(conv_inner.shape)
    stepbias_grad = small[:, 0, mix : mix + heads].reshape(-1)
    decay_grad = small[:, 1, mix : mix + heads].reshape(-1)
    skip_grad = jnp.sum(small[:, 0, at : at + width].reshape(ranks * heads, PD), axis=1)
    mgain_grad = small[:, 1, at : at + width].reshape(-1)
    shared_small = jnp.sum(small, axis=0)
    convst_grad = shared_small[: CONV + 1, width:mix].reshape(conv_state.shape)
    at = at + width
    norm_columns = norm1_part.shape[0] // 8
    norm1_grad = shared_small[:, at : at + norm_columns].reshape(-1)
    norm2_grad = shared_small[:, at + norm_columns :].reshape(-1)
    return (
        layer_out,
        tokens_grad,
        norm1_grad,
        norm2_grad,
        query_grad,
        keyval_grad,
        attn_grad,
        inner_grad,
        state_grad,
        step_grad,
        convin_grad,
        convst_grad,
        stepbias_grad,
        decay_grad,
        skip_grad,
        mgain_grad,
        mamba_grad,
        gateup_grad,
        down_grad,
    )


def solution(mesh):
    rows_split = P(("dp", "ctx"), None)
    split_0 = P(("dp", "ctx"), "tp")
    split_0_whole = P(("dp", "ctx"), None, None)
    split_0_last = P(("dp", "ctx"), None, "tp")
    split_1 = P("tp", ("dp", "ctx"))
    return jax.shard_map(
        body,
        mesh=mesh,
        in_specs=(
            rows_split,
            rows_split,
            P("dp", None),
            P(),
            P(),
            split_0,
            split_0_whole,
            split_1,
            split_0_last,
            split_0_whole,
            split_0,
            P(),
            P(),
            P(),
            P(),
            P(),
            P(),
            split_1,
            split_0_last,
            split_1,
        ),
        out_specs=(
            rows_split,
            rows_split,
            P(),
            P(),
            split_0,
            split_0_whole,
            split_1,
            split_0_last,
            split_0_whole,
            split_0,
            P(),
            P(),
            P(),
            P(),
            P(),
            P(),
            split_1,
            split_0_last,
            split_1,
        ),
        check_vma=False,
    )
```

```python
import functools

import jax
import jax.numpy as jnp
from jax import lax
from jax.experimental import pallas as pl
from jax.experimental.layout import Layout, with_layout_constraint
from jax.experimental.pallas import tpu as pltpu
from jax.sharding import PartitionSpec as P

H = 8
KVH = 2
HD = 64
PD = 64
NST = 128
CONV = 4
CHUNK = 256
QUERY_BLOCK = 256
KEY_BLOCK = 512
EDGE = 8
LANES = 128
VMEM_BYTES = 48 * 1024 * 1024

EPS = 1e-05
ROPE_BASE = 10000.0
MASKED = -1e30
HIGH = lax.Precision.HIGHEST
F32 = jnp.float32
BF16 = jnp.bfloat16
WEIGHT_AXES = ("dp", "ctx")


def product(left, right):
    return jnp.dot(left, right, preferred_element_type=F32)


def product_tn(left, right):
    return lax.dot_general(left, right, (((0,), (0,)), ((), ())), preferred_element_type=F32)


def product_nt(left, right):
    return lax.dot_general(left, right, (((1,), (1,)), ((), ())), preferred_element_type=F32)


def low_nn(left, right):
    return product(left.astype(BF16), right.astype(BF16))


def low_tn(left, right):
    return product_tn(left.astype(BF16), right.astype(BF16))


def low_nt(left, right):
    return product_nt(left.astype(BF16), right.astype(BF16))


def split_nn(left, ones):
    first = left.astype(BF16)
    second = (left - first.astype(F32)).astype(BF16)
    return product(first, ones) + product(second, ones)


def split_nt(ones, right):
    first = right.astype(BF16)
    second = (right - first.astype(F32)).astype(BF16)
    return product_nt(ones, first) + product_nt(ones, second)


def iota(shape, dim):
    return lax.broadcasted_iota(jnp.int32, shape, dim)


def start_of(rows, meta, docs):
    start = jnp.full(rows.shape, meta[0], jnp.int32)
    for doc in range(1, docs):
        start = jnp.where(rows >= meta[doc], meta[doc], start)
    return start


def start_of_one(row, meta, docs):
    start = meta[0]
    for doc in range(1, docs):
        start = jnp.where(row >= meta[doc], meta[doc], start)
    return start


def sigmoid(values):
    return 1.0 / (1.0 + jnp.exp(-values))


def swap_halves(values):
    lane = iota(values.shape, 1)
    up = pltpu.roll(values, LANES - HD // 2, 1)
    down = pltpu.roll(values, HD // 2, 1)
    return jnp.where(lane % HD < HD // 2, up, down)


def prep_kernel(
    docs,
    inner_width,
    meta,
    proj,
    edge,
    taps,
    heads,
    cosine,
    sine,
    spread,
    spread_t,
    q_out,
    kv_out,
    mixed_out,
    act_out,
    slope_out,
    step_out,
    sig_out,
    cum_out,
    state_out,
    end_out,
    ext,
    state,
    total_log,
):
    c = pl.program_id(0)
    rows = proj.shape[0]
    mix = ext.shape[1]
    row = c * rows + iota((rows, 1), 0)
    rel = row - start_of(row, meta, docs)
    mixed = proj[:, :mix].astype(BF16)
    mixed_out[...] = mixed

    @pl.when(c == 0)
    def _():
        ext[0:EDGE] = edge[...]
        state[...] = jnp.zeros_like(state)
        total_log[...] = jnp.zeros_like(total_log)

    @pl.when(c > 0)
    def _():
        ext[0:EDGE] = ext[rows : rows + EDGE]

    ext[EDGE : EDGE + rows] = mixed.astype(F32)
    pre = jnp.broadcast_to(taps[CONV : CONV + 1, :], (rows, mix))
    for lag in range(CONV):
        keep = (rel >= lag).astype(F32)
        pre = pre + taps[CONV - 1 - lag : CONV - lag, :] * (
            ext[EDGE - lag : EDGE - lag + rows] * keep
        )
    sig = sigmoid(pre)
    act = pre * sig
    act_out[...] = act
    slope_out[...] = sig * (1.0 + pre * (1.0 - sig))

    base = mix
    cos, sin = (cosine[...], sine[...])
    queries = proj[:, base : base + LANES]
    turned = queries * cos + swap_halves(queries) * sin
    q_out[...] = (turned * HD ** (-0.5)).astype(BF16)
    keyval = proj[:, base + LANES : base + 2 * LANES]
    is_key = iota(keyval.shape, 1) < HD
    kv_out[...] = jnp.where(is_key, keyval * cos + swap_halves(keyval) * sin, keyval).astype(BF16)

    raw = proj[:, base + 2 * LANES : base + 3 * LANES] + heads[0:1, :]
    step = jnp.maximum(raw, 0.0) + jnp.log1p(jnp.exp(-jnp.abs(raw)))
    decay = -step * heads[1:2, :]
    lower = (iota((rows, rows), 0) >= iota((rows, rows), 1)).astype(F32)
    cum = jnp.dot(lower, decay, precision=HIGH, preferred_element_type=F32)
    step_out[...] = step
    sig_out[...] = sigmoid(raw)
    cum_out[...] = cum

    last = c * rows + rows - 1
    last_start = start_of_one(last, meta, docs)
    total = cum[rows - 1 : rows, :]
    tail = jnp.where(row >= last_start, jnp.exp(total - cum), 0.0) * step
    goes_on = jnp.where(last_start < c * rows, 1.0, 0.0)
    kept = split_nt(spread_t[...], jnp.broadcast_to(jnp.exp(total) * goes_on, (NST, LANES)))
    state_out[...] = state[...]
    added = low_tn(act[:, :inner_width] * split_nn(tail, spread[...]), act[:, inner_width : inner_width + NST])
    state[...] = kept * state[...] + added
    total_log[...] = total_log[...] + jnp.broadcast_to(total, total_log.shape)

    @pl.when(c == pl.num_programs(0) - 1)
    def _():
        through = jnp.exp(total_log[0:1, :]) * jnp.where(last_start < 0, 1.0, 0.0)
        first = through.astype(BF16)
        second = (through - first.astype(F32)).astype(BF16)
        sub = iota((16, LANES), 0)
        end_out[0:inner_width] = state[...].astype(BF16)
        end_out[inner_width : inner_width + 16] = jnp.where(
            sub == 0, first.astype(F32), jnp.where(sub == 1, second.astype(F32), 0.0)
        ).astype(BF16)


def intra_kernel(docs, inner_width, meta, act, step, cum, spread, y_out):
    c = pl.program_id(0)
    rows = act.shape[0]
    row = iota((rows, 1), 0)
    first = start_of(c * rows + row, meta, docs) - c * rows
    col = iota((rows, rows), 1)
    linked = (col >= first) & (col <= iota((rows, rows), 0))
    couple = low_nt(act[:, inner_width + NST :], act[:, inner_width : inner_width + NST])
    weighted = (act[:, :inner_width] * split_nn(step[...], spread[...])).astype(BF16)
    cum_now = cum[...]
    cum_t = cum_now.T
    lane = iota((rows, LANES), 1)
    for pair in range(inner_width // LANES):
        values = weighted[:, pair * LANES : (pair + 1) * LANES]
        results = []
        for head in (2 * pair, 2 * pair + 1):
            arg = cum_now[:, head : head + 1] - cum_t[head : head + 1, :]
            mixing = couple * jnp.exp(jnp.where(linked, arg, MASKED))
            results.append(product(mixing.astype(BF16), values))
        y_out[:, pair * LANES : (pair + 1) * LANES] = jnp.where(lane < PD, results[0], results[1])


def two_heads(values, upper):
    values = values.astype(F32)
    lane = iota(values.shape, 1)
    rolled = pltpu.roll(values, HD, 1)
    keep = lane >= HD if upper else lane < HD
    pair = (rolled, values) if upper else (values, rolled)
    return jnp.concatenate([jnp.where(keep, part, 0.0) for part in pair], axis=0)


def attend_kernel(docs, meta, q, kv, out, lse_out):
    block = pl.program_id(0)
    rows = q.shape[0]
    first_row = meta[docs]
    row = block * rows + iota((rows, 1), 0)
    start = start_of(row, meta, docs)
    queries = two_heads(q[...], False).astype(BF16)
    low_block = (start_of_one(block * rows, meta, docs) + first_row) // KEY_BLOCK
    high_block = (first_row + (block + 1) * rows + KEY_BLOCK - 1) // KEY_BLOCK

    def one(index, sums):
        top, total, summed = sums
        at = pl.multiple_of(index * KEY_BLOCK, KEY_BLOCK)
        keyval = kv[pl.ds(at, KEY_BLOCK), :]
        scores = product_nt(queries, keyval)
        key = index * KEY_BLOCK - first_row + iota((rows, KEY_BLOCK), 1)
        allowed = (key >= start) & (key <= row)
        allowed = jnp.concatenate([allowed, allowed], axis=0)
        scores = jnp.where(allowed, scores, MASKED)
        new_top = jnp.maximum(top, jnp.max(scores, axis=1, keepdims=True))
        scale = jnp.exp(top - new_top)
        probs = jnp.exp(scores - new_top)
        total = total * scale + jnp.sum(probs, axis=1, keepdims=True)
        return (new_top, total, summed * scale + product(probs.astype(BF16), keyval))

    top, total, summed = lax.fori_loop(
        low_block,
        high_block,
        one,
        (
            jnp.full((2 * rows, 1), MASKED, F32),
            jnp.zeros((2 * rows, 1), F32),
            jnp.zeros((2 * rows, LANES), F32),
        ),
    )
    result = summed / total
    lse = top + jnp.log(total)
    lane = iota((rows, LANES), 1)
    out[...] = jnp.where(lane < HD, pltpu.roll(result[:rows], HD, 1), result[rows:]).astype(BF16)
    lse_out[...] = jnp.where(lane < HD, lse[:rows], lse[rows:])


def attend_back_kernel(docs, meta, q, kv, grad, att, lse, cosine, sine, gq_out, gkv_out):
    block = pl.program_id(0)
    rows = q.shape[0]
    first_row = meta[docs]

    @pl.when(block == 0)
    def _():
        gkv_out[...] = jnp.zeros_like(gkv_out)

    row = block * rows + iota((rows, 1), 0)
    start = start_of(row, meta, docs)
    queries = two_heads(q[...], False).astype(BF16)
    grads = two_heads(grad[...].astype(BF16), True)
    lse_now = lse[...]
    lse_col = jnp.concatenate([lse_now[:, 0:1], lse_now[:, HD : HD + 1]], axis=0)
    delta = jnp.sum(grads * two_heads(att[...], True), axis=1, keepdims=True)
    grads = grads.astype(BF16)
    low_block = (start_of_one(block * rows, meta, docs) + first_row) // KEY_BLOCK
    high_block = (first_row + (block + 1) * rows + KEY_BLOCK - 1) // KEY_BLOCK

    def one(index, summed):
        at = pl.multiple_of(index * KEY_BLOCK, KEY_BLOCK)
        keyval = kv[pl.ds(at, KEY_BLOCK), :]
        scores = product_nt(queries, keyval)
        key = index * KEY_BLOCK - first_row + iota((rows, KEY_BLOCK), 1)
        allowed = (key >= start) & (key <= row)
        allowed = jnp.concatenate([allowed, allowed], axis=0)
        probs = jnp.exp(jnp.where(allowed, scores - lse_col, MASKED))
        grad_scores = (probs * (product_nt(grads, keyval) - delta)).astype(BF16)
        gkv_out[pl.ds(at, KEY_BLOCK), :] += product_tn(grad_scores, queries) + product_tn(
            probs.astype(BF16), grads
        )
        return summed + product(grad_scores, keyval)

    summed = lax.fori_loop(low_block, high_block, one, jnp.zeros((2 * rows, LANES), F32))
    lane = iota((rows, LANES), 1)
    grad_q = jnp.where(lane < HD, summed[:rows], pltpu.roll(summed[rows:], HD, 1)) * HD ** (-0.5)
    gq_out[...] = (grad_q * cosine[...] - swap_halves(grad_q) * sine[...]).astype(BF16)


def finish_kernel(
    docs,
    inner_width,
    meta,
    y_in,
    act,
    cum,
    gate,
    att,
    state_local,
    state_in,
    params,
    spread,
    spread_t,
    block_ones,
    low_out,
    y_out,
    state_out,
    carry,
):
    c = pl.program_id(0)
    rows = act.shape[0]

    @pl.when(c == 0)
    def _():
        carry[...] = state_in[...]

    row = c * rows + iota((rows, 1), 0)
    start = start_of(row, meta, docs)
    last_start = start_of_one(c * rows + rows - 1, meta, docs)
    cum_now = cum[...]
    inflow = jnp.where(start < c * rows, jnp.exp(cum_now), 0.0)
    state = state_local[...] + carry[...]
    state_out[...] = state
    inner = act[:, :inner_width]
    y = y_in[...] + low_nt(act[:, inner_width + NST :], state) * split_nn(inflow, spread[...])
    y_out[...] = y
    total = jnp.exp(cum_now[rows - 1 : rows, :]) * jnp.where(last_start < c * rows, 1.0, 0.0)
    carry[...] = carry[...] * split_nt(spread_t[...], jnp.broadcast_to(total, (NST, LANES)))
    gate_now = gate[...]
    gated = (y + params[0:1, :] * inner) * (gate_now * sigmoid(gate_now))
    mean = split_nn(gated * gated, block_ones[...]) * (1.0 / PD)
    low = gated * lax.rsqrt(mean + EPS) * params[1:2, :]
    low_out[:, :LANES] = att[...]
    low_out[:, LANES:] = low.astype(BF16)


def finish_back_kernel(
    docs,
    inner_width,
    meta,
    grad,
    y_in,
    act,
    cum,
    gate,
    params,
    spread,
    block_ones,
    gy_out,
    gate_out,
    params_out,
    state_out,
    so_far,
):
    c = pl.program_id(0)
    rows = act.shape[0]

    @pl.when(c == 0)
    def _():
        params_out[...] = jnp.zeros_like(params_out)
        state_out[...] = jnp.zeros_like(state_out)
        so_far[...] = jnp.zeros_like(so_far)

    row = c * rows + iota((rows, 1), 0)
    start = start_of(row, meta, docs)
    cum_now = cum[...]
    inner = act[:, :inner_width]
    skip, gain = (params[0:1, :], params[1:2, :])
    gate_now = gate[...]
    sig = sigmoid(gate_now)
    silu = gate_now * sig
    with_skip = y_in[...] + skip * inner
    gated = with_skip * silu
    ones = block_ones[...]
    scale = lax.rsqrt(split_nn(gated * gated, ones) * (1.0 / PD) + EPS)
    grad_now = grad[...]
    unit = gated * scale
    grad_unit = grad_now * gain
    mean = split_nn(grad_unit * unit, ones) * (1.0 / PD)
    grad_gated = scale * (grad_unit - unit * mean)
    grad_y = grad_gated * silu
    gy_out[...] = grad_y
    gate_out[...] = (grad_gated * with_skip * (sig * (1.0 + gate_now * (1.0 - sig)))).astype(BF16)
    params_out[0:1, :] += jnp.sum(grad_y * inner, axis=0, keepdims=True)
    params_out[1:2, :] += jnp.sum(grad_now * unit, axis=0, keepdims=True)
    inflow = jnp.where(start < 0, jnp.exp(cum_now + so_far[0:1, :]), 0.0)
    state_out[...] += low_tn(grad_y * split_nn(inflow, spread[...]), act[:, inner_width + NST :])
    so_far[...] = so_far[...] + jnp.broadcast_to(cum_now[rows - 1 : rows, :], so_far.shape)


def scan_back_kernel(
    docs,
    inner_width,
    meta,
    act,
    slope,
    step_in,
    sig_in,
    cum,
    grad_y_in,
    state_in,
    grad_end,
    mixed,
    edge,
    taps,
    heads,
    params,
    spread,
    spread_t,
    gmix_out,
    gstep_out,
    tail_out,
    edge_out,
    taps_out,
    heads_out,
    ext,
    grad_state,
):
    c = pl.num_programs(0) - 1 - pl.program_id(0)
    rows = act.shape[0]

    @pl.when(pl.program_id(0) == 0)
    def _():
        grad_state[...] = grad_end[...]
        ext[0:EDGE] = jnp.zeros((EDGE, ext.shape[1]), F32)
        ext[EDGE + rows :] = jnp.zeros((EDGE, ext.shape[1]), F32)
        taps_out[...] = jnp.zeros_like(taps_out)
        heads_out[...] = jnp.zeros_like(heads_out)

    @pl.when(pl.program_id(0) > 0)
    def _():
        ext[EDGE + rows :] = ext[EDGE : 2 * EDGE]

    at = c * rows
    row = at + iota((rows, 1), 0)
    start = start_of(row, meta, docs)
    last_start = start_of_one(at + rows - 1, meta, docs)
    inner = act[:, :inner_width]
    write = act[:, inner_width : inner_width + NST].astype(BF16)
    read = act[:, inner_width + NST :].astype(BF16)
    step = step_in[...]
    cum_now = cum[...]
    grad_y = grad_y_in[...]
    spread_now = spread[...]
    spread_back = spread_t[...]
    state = state_in[...]
    grads = grad_state[...]
    total = cum_now[rows - 1 : rows, :]
    step_wide = split_nn(step, spread_now)
    weighted = inner * step_wide
    tail = split_nn(jnp.where(row >= last_start, jnp.exp(total - cum_now), 0.0), spread_now)
    inflow = split_nn(jnp.where(start < at, jnp.exp(cum_now), 0.0), spread_now)
    kept_row = jnp.exp(total) * jnp.where(last_start < at, 1.0, 0.0)

    grads_low = grads.astype(BF16)
    state_low = state.astype(BF16)
    from_state = tail * product_nt(write, grads_low)
    leaving = split_nn(weighted * from_state, spread_back)
    grad_write = low_nn(tail * weighted, grads_low)
    arriving_y = inflow * grad_y
    arriving_low = arriving_y.astype(BF16)
    grad_read = product(arriving_low, state_low)
    arriving = split_nn(arriving_y * product_nt(read, state_low), spread_back)
    grad_state[...] = split_nt(
        spread_back, jnp.broadcast_to(kept_row, (NST, LANES))
    ) * grads + product_tn(arriving_low, read)
    both = split_nt(jnp.ones((8, NST), BF16), grads * state)
    kept_grad = kept_row * split_nn(both, spread_back)[0:1, :]
    grad_total = kept_grad + jnp.sum(leaving, axis=0, keepdims=True)

    couple_t = product_nt(write, read)
    at_key = iota((rows, rows), 0)
    at_query = iota((rows, rows), 1)
    end_row = at + iota((1, rows), 1)
    start_row = start_of(end_row, meta, docs) - at
    linked = (at_key >= start_row) & (at_key <= at_query)
    cum_t = cum_now.T
    lane = iota((rows, LANES), 1)
    sub = iota((LANES, rows), 0)
    weighted_low = weighted.astype(BF16)
    grad_y_low = grad_y.astype(BF16)
    grad_couple = jnp.zeros((rows, rows), F32)
    grad_cum = arriving - leaving
    grad_cum_t = jnp.zeros((LANES, rows), F32)
    pieces = []
    for pair in range(inner_width // LANES):
        span = slice(pair * LANES, (pair + 1) * LANES)
        values = weighted_low[:, span]
        grads_here = grad_y_low[:, span]
        results = []
        for side in range(2):
            head = 2 * pair + side
            arg = cum_t[head : head + 1, :] - cum_now[:, head : head + 1]
            decay = jnp.exp(jnp.where(linked, arg, MASKED))
            mine = jnp.where((lane >= PD) == (side == 1), values, jnp.zeros_like(values))
            grad_mixing = product_nt(mine, grads_here) * decay
            grad_couple = grad_couple + grad_mixing
            by_log = grad_mixing * couple_t
            grad_cum = grad_cum - jnp.where(
                lane == head, jnp.sum(by_log, axis=1, keepdims=True), 0.0
            )
            grad_cum_t = grad_cum_t + jnp.where(
                sub == head, jnp.sum(by_log, axis=0, keepdims=True), 0.0
            )
            results.append(product((couple_t * decay).astype(BF16), grads_here))
        pieces.append(jnp.where(lane < PD, results[0], results[1]))
    grad_weighted = jnp.concatenate(pieces, axis=1) + from_state
    grad_couple_low = grad_couple.astype(BF16)
    grad_write = grad_write + product(grad_couple_low, read)
    grad_read = grad_read + product_tn(grad_couple_low, write)

    grad_cum = grad_cum + grad_cum_t.T
    upper = (at_query >= at_key).astype(F32)
    grad_decay = (
        jnp.dot(upper, grad_cum, precision=HIGH, preferred_element_type=F32) + grad_total
    )
    rate = heads[1:2, :]
    grad_inner = grad_weighted * step_wide + grad_y * params[0:1, :]
    grad_step = split_nn(grad_weighted * inner, spread_back) - grad_decay * rate
    grad_raw = grad_step * sig_in[...]
    gstep_out[...] = grad_raw.astype(BF16)
    heads_out[0:1, :] += jnp.sum(grad_raw, axis=0, keepdims=True)
    heads_out[1:2, :] += jnp.sum(grad_decay * (-step * rate), axis=0, keepdims=True)

    grad_pre = jnp.concatenate([grad_inner, grad_write, grad_read], axis=1) * slope[...]
    ext[EDGE : EDGE + rows] = grad_pre
    taps_out[CONV : CONV + 1, :] += jnp.sum(grad_pre, axis=0, keepdims=True)
    mixed_now = mixed[...].astype(F32)
    grad_mixed = jnp.zeros_like(grad_pre)
    for lag in range(CONV):
        target = row + lag
        keep = (target - start_of(target, meta, docs) >= lag).astype(F32)
        moved = ext[EDGE + lag : EDGE + lag + rows] * keep
        grad_mixed = grad_mixed + taps[CONV - 1 - lag : CONV - lag, :] * moved
        taps_out[CONV - 1 - lag : CONV - lag, :] += jnp.sum(
            moved * mixed_now, axis=0, keepdims=True
        )
    gmix_out[...] = grad_mixed.astype(BF16)

    @pl.when(pl.program_id(0) == 0)
    def _():
        tail_out[...] = grad_mixed[rows - EDGE :]

    @pl.when(c == 0)
    def _():
        before = iota((EDGE, 1), 0) - EDGE
        edge_now = edge[...]
        grad_edge = jnp.zeros_like(edge_now)
        for lag in range(1, CONV):
            target = before + lag
            keep = (target - start_of(target, meta, docs) >= lag).astype(F32)
            moved = ext[lag : lag + EDGE] * keep
            grad_edge = grad_edge + taps[CONV - 1 - lag : CONV - lag, :] * moved
            taps_out[CONV - 1 - lag : CONV - lag, :] += jnp.sum(
                moved * edge_now, axis=0, keepdims=True
            )
        edge_out[...] = grad_edge


def feed_kernel(ff, normed, cotangent, weights, act_out, grad_out, back_out, forward_out):
    gateup_w = weights[:, : 2 * ff]
    down_w = weights[:, 2 * ff :]
    grad_hidden = product(cotangent[...], down_w)
    gateup = product(normed[...], gateup_w)
    gate, up = (gateup[:, :ff], gateup[:, ff:])
    sig = sigmoid(gate)
    silu = gate * sig
    act = (silu * up).astype(BF16)
    act_out[...] = act
    grad_gate = grad_hidden * up * (sig * (1.0 + gate * (1.0 - sig)))
    grad = jnp.concatenate([grad_gate, grad_hidden * silu], axis=1).astype(BF16)
    grad_out[...] = grad
    back_out[...] = product_nt(grad, gateup_w).astype(BF16)
    forward_out[...] = product_nt(act, down_w).astype(BF16)


def call(kernel, grid, ins, outs, scratch=()):
    def spec(shape, block, index):
        if block == "any":
            return pl.BlockSpec(memory_space=pl.ANY)
        if block == "smem":
            return pl.BlockSpec(memory_space=pltpu.SMEM)
        if block is None:
            return pl.BlockSpec(shape, lambda i: (0,) * len(shape))
        return pl.BlockSpec(block, index)

    return pl.pallas_call(
        kernel,
        grid=(grid,),
        in_specs=[spec(a.shape, block, index) for a, block, index in ins],
        out_specs=[spec(shape, block, index) for shape, _, block, index in outs],
        out_shape=[jax.ShapeDtypeStruct(shape, kind) for shape, kind, _, _ in outs],
        scratch_shapes=list(scratch),
        compiler_params=pltpu.CompilerParams(
            dimension_semantics=("arbitrary",), vmem_limit_bytes=VMEM_BYTES
        ),
    )(*[a for a, _, _ in ins])


def pass_kernel(*refs):
    del refs


def after(values, *others):
    anywhere = pl.BlockSpec(memory_space=pl.ANY)
    return pl.pallas_call(
        pass_kernel,
        in_specs=[anywhere] * (1 + len(others)),
        out_specs=anywhere,
        out_shape=jax.ShapeDtypeStruct(values.shape, values.dtype),
        input_output_aliases={0: 0},
    )(values, *others)


def by_row(i):
    return (i, 0)


def exchange(values, axis, step):
    return lax.ppermute(values, axis, [(k, k ^ step) for k in range(lax.axis_size(axis))])


def bits_of(axis):
    return (lax.axis_size(axis) - 1).bit_length()


def bit_of(axis, bit):
    return (lax.axis_index(axis) >> bit) & 1


def halved(values, axis, at, bit):
    shape = values.shape
    values = values.reshape(shape[:at] + (shape[at] // 2, 2) + shape[at + 1 :])
    mine = bit_of(axis, bit)
    kept = lax.dynamic_index_in_dim(values, mine, at + 1, False)
    sent = lax.dynamic_index_in_dim(values, 1 - mine, at + 1, False)
    return (kept.astype(F32) + exchange(sent, axis, 1 << bit).astype(F32)).astype(BF16)


def scattered(values, axis, at, first_bit=0):
    for bit in range(first_bit, bits_of(axis)):
        values = halved(values, axis, at, bit)
    return lax.squeeze(values, (at,))


def gathered(values, axis):
    bits = bits_of(axis)
    for place, bit in enumerate(reversed(range(bits))):
        other = exchange(values, axis, 1 << bit)
        upper = bit_of(axis, bit) == 1
        values = jnp.stack(
            [jnp.where(upper, other, values), jnp.where(upper, values, other)], axis=place
        )
    shape = values.shape[bits:]
    return values.reshape((lax.axis_size(axis),) + shape)


def summed_over(values, axes):
    for axis in axes:
        for bit in range(bits_of(axis)):
            values = values + exchange(values, axis, 1 << bit)
    return values


class Owned:
    def __init__(self, terms, along):
        dp, ctx = (lax.axis_size(name) for name in WEIGHT_AXES)
        rows, columns = terms.shape
        self.shape = (rows // (dp * ctx), columns)
        self.values = terms.astype(BF16).reshape((dp, ctx) + self.shape)
        over_ctx = [("ctx", 1, bit) for bit in range(bits_of("ctx"))]
        over_dp = [("dp", 0, bit) for bit in range(bits_of("dp"))]
        self.steps = over_ctx + over_dp if along == "ctx" else over_dp + over_ctx

    def step(self):
        if self.steps:
            self.values = halved(self.values, *self.steps.pop(0))

    def result(self):
        while self.steps:
            self.step()
        return self.values.reshape(self.shape).astype(F32)


def chain(gathered, order, width, heads, reached):
    state = jnp.zeros((width, NST), F32)
    for k in order:
        own = gathered[k, :width].astype(F32)
        through = gathered[k, width].astype(F32) + gathered[k, width + 1].astype(F32)
        wide = jnp.repeat(through[:heads], PD)[:, None]
        state = jnp.where(reached(k), wide * state + own, state)
    return state


def rms_scale(values, gain):
    return values * lax.rsqrt(jnp.mean(values * values, axis=-1, keepdims=True) + EPS) * gain


def rms_back(values, gain, grad):
    scale = lax.rsqrt(jnp.mean(values * values, axis=-1, keepdims=True) + EPS)
    unit = values * scale
    inner = jnp.mean(grad * gain * values, axis=-1, keepdims=True)
    return (scale * (grad * gain - values * scale * scale * inner), jnp.sum(grad * unit, axis=0))


def body(
    tokens,
    cotangent,
    lengths,
    norm1_gain,
    norm2_gain,
    query_proj,
    keyval_proj,
    attn_proj,
    inner_proj,
    state_proj,
    step_proj,
    conv_inner,
    conv_state,
    step_bias,
    decay_log,
    skip_gain,
    mamba_gain,
    mamba_proj,
    gateup_proj,
    down_proj,
):
    rows = tokens.shape[0]
    rank = lax.axis_index("tp")
    ranks = lax.axis_size("tp")
    ctx_rank = lax.axis_index("ctx")
    ctx_size = lax.axis_size("ctx")
    pack = rows * ctx_size
    shard = query_proj.shape[0]
    width = inner_proj.shape[2]
    heads = width // PD
    mix = width + 2 * NST
    ff = gateup_proj.shape[2]
    docs = lengths.shape[1]
    quarter = rows // ranks
    chunks = rows // CHUNK
    kv_head = rank * (query_proj.shape[1] // HD) // (H // KVH)

    kv_heads = keyval_proj.reshape(shard, 2, KVH, HD)
    kv_shard = kv_heads[:, :, 0]
    for head in range(1, KVH):
        kv_shard = jnp.where(kv_head == head, kv_heads[:, :, head], kv_shard)
    kv_shard = kv_shard.reshape(shard, 2 * HD)
    step_shard = jnp.pad(step_proj, ((0, 0), (0, LANES - heads)))
    inner_shard = inner_proj.reshape(shard, 2 * width)
    first_shard = jnp.concatenate(
        [inner_shard[:, width:], state_proj.reshape(shard, 2 * NST), query_proj, kv_shard, step_shard],
        axis=1,
    )
    mixer_shard = jnp.concatenate([inner_shard[:, :width], attn_proj.T, mamba_proj.T], axis=1)
    last_shard = jnp.concatenate([gateup_proj.reshape(shard, 2 * ff), down_proj.T], axis=1)

    def whole(part):
        return lax.all_gather(part, WEIGHT_AXES, axis=0, tiled=True)

    first_w = whole(first_shard)
    second_w = whole(mixer_shard)
    gate_w = second_w[:, :width]
    mixer_w = second_w[:, width:]
    last_w = whole(last_shard)

    first_row = ctx_rank * rows
    bounds = jnp.cumsum(lengths[0])
    starts = bounds - lengths[0] - first_row
    meta = jnp.concatenate([starts, first_row[None]]).astype(jnp.int32)
    local = jnp.arange(rows, dtype=jnp.int32)
    doc_start = jnp.max(
        jnp.where(local[:, None] >= starts[None, :], starts[None, :], starts[0]), axis=1
    )
    frequency = ROPE_BASE ** (-jnp.arange(HD // 2, dtype=F32) / (HD // 2))
    angles = (local - doc_start).astype(F32)[:, None] * jnp.tile(frequency, 4)[None, :]
    sign = jnp.where(jnp.arange(LANES) % HD < HD // 2, -1.0, 1.0).astype(F32)
    cosine = jnp.cos(angles)
    sine = jnp.sin(angles) * sign[None, :]

    def mine(values, size, axis):
        return lax.dynamic_slice_in_dim(values, rank * size, size, axis)

    taps = jnp.concatenate([mine(conv_inner, width, 1), conv_state.reshape(CONV + 1, -1)], axis=1)
    taps = jnp.pad(taps, ((0, 8 - (CONV + 1)), (0, 0)))
    bias = mine(step_bias, heads, 0)
    rate = jnp.exp(mine(decay_log, heads, 0))
    head_params = jnp.pad(jnp.stack([bias, rate]), ((0, 6), (0, LANES - heads)))
    params = jnp.pad(
        jnp.stack([jnp.repeat(mine(skip_gain, heads, 0), PD), mine(mamba_gain, width, 0)]),
        ((0, 6), (0, 0)),
    )
    channel_head = jnp.arange(width) // PD
    spread = (jnp.arange(LANES)[:, None] == channel_head[None, :]).astype(BF16)
    spread_t = spread.T
    block_ones = (channel_head[:, None] == channel_head[None, :]).astype(BF16)

    normed = lax.optimization_barrier(rms_scale(tokens.astype(F32), norm1_gain).astype(BF16))
    onward = [(source, source + 1) for source in range(ctx_size - 1)]
    backward = [(source + 1, source) for source in range(ctx_size - 1)]
    edge_tokens = lax.ppermute(tokens[rows - EDGE :], "ctx", onward).astype(F32)
    edge_normed = rms_scale(edge_tokens, norm1_gain).astype(BF16)
    proj = product(normed, first_w)
    edge = product(edge_normed, first_w[:, :mix]).astype(BF16).astype(F32)

    chunk_128 = (CHUNK, LANES)
    chunk_mix = (CHUNK, mix)
    chunk_width = (CHUNK, width)
    q_rot, kv_local, mixed, act, slope, step, sig, cum, state_local, end = call(
        functools.partial(prep_kernel, docs, width),
        chunks,
        [
            (meta, "smem", None),
            (proj, (CHUNK, proj.shape[1]), by_row),
            (edge, None, None),
            (taps, None, None),
            (head_params, None, None),
            (cosine, chunk_128, by_row),
            (sine, chunk_128, by_row),
            (spread, None, None),
            (spread_t, None, None),
        ],
        [
            ((rows, LANES), BF16, chunk_128, by_row),
            ((rows, LANES), BF16, chunk_128, by_row),
            ((rows, mix), BF16, chunk_mix, by_row),
            ((rows, mix), F32, chunk_mix, by_row),
            ((rows, mix), F32, chunk_mix, by_row),
            ((rows, LANES), F32, chunk_128, by_row),
            ((rows, LANES), F32, chunk_128, by_row),
            ((rows, LANES), F32, chunk_128, by_row),
            ((chunks * width, NST), F32, (width, NST), by_row),
            ((width + 16, NST), BF16, None, None),
        ],
        [
            pltpu.VMEM((CHUNK + EDGE, mix), F32),
            pltpu.VMEM((width, NST), F32),
            pltpu.VMEM((8, LANES), F32),
        ],
    )
    ends = gathered(end, "ctx")
    kv_all = gathered(kv_local, "ctx").reshape(pack, LANES)
    (y_intra,) = call(
        functools.partial(intra_kernel, docs, width),
        chunks,
        [
            (meta, "smem", None),
            (act, chunk_mix, by_row),
            (step, chunk_128, by_row),
            (cum, chunk_128, by_row),
            (spread, None, None),
        ],
        [((rows, width), F32, chunk_width, by_row)],
    )
    blocks = rows // QUERY_BLOCK
    block_128 = (QUERY_BLOCK, LANES)
    attended, lse = call(
        functools.partial(attend_kernel, docs),
        blocks,
        [(meta, "smem", None), (q_rot, block_128, by_row), (kv_all, None, None)],
        [((rows, LANES), BF16, block_128, by_row), ((rows, LANES), F32, block_128, by_row)],
    )
    normed_again, _ = lax.optimization_barrier((normed, (attended, y_intra)))
    gate_z = product(normed_again, gate_w)
    state_in = chain(ends, range(ctx_size - 1), width, heads, lambda k: k < ctx_rank)
    mixer_low, y, states = call(
        functools.partial(finish_kernel, docs, width),
        chunks,
        [
            (meta, "smem", None),
            (y_intra, chunk_width, by_row),
            (act, chunk_mix, by_row),
            (cum, chunk_128, by_row),
            (gate_z, chunk_width, by_row),
            (attended, chunk_128, by_row),
            (state_local, (width, NST), by_row),
            (state_in, None, None),
            (params, None, None),
            (spread, None, None),
            (spread_t, None, None),
            (block_ones, None, None),
        ],
        [
            ((rows, LANES + width), BF16, (CHUNK, LANES + width), by_row),
            ((rows, width), F32, chunk_width, by_row),
            ((chunks * width, NST), F32, (width, NST), by_row),
        ],
        [pltpu.VMEM((width, NST), F32)],
    )

    def scatter_rows(values, first_after=(), then_after=()):
        values, _ = lax.optimization_barrier((values, first_after))
        values = values.reshape(ranks, quarter, values.shape[1])
        values = halved(values, "tp", 0, 0)
        values, _ = lax.optimization_barrier((values, then_after))
        return scattered(values, "tp", 0, 1).astype(F32)

    def scatter_product(left, right):
        halves = left.reshape(ranks // 2, 2, quarter, left.shape[1])

        def half(which):
            chosen = lax.dynamic_index_in_dim(halves, which, 1, False)
            return product_nt(chosen.reshape(-1, left.shape[1]), right).astype(BF16)

        bit = bit_of("tp", 0)
        sent, kept = lax.optimization_barrier((half(1 - bit), half(bit)))
        values = kept.astype(F32) + exchange(sent, "tp", 1).astype(F32)
        values = values.astype(BF16).reshape(ranks // 2, quarter, right.shape[0])
        return values, lambda: scattered(values, "tp", 0, 1).astype(F32)

    def row_major(values):
        return with_layout_constraint(values, Layout(major_to_minor=(0, 1)))

    def gather_rows(values):
        return gathered(values, "tp").reshape(rows, values.shape[1])

    hidden_q = mine(tokens, quarter, 0).astype(F32)
    residual = hidden_q + scatter_product(mixer_low, mixer_w)[1]()
    normed2 = gather_rows(rms_scale(residual, norm2_gain).astype(BF16))
    row_block = (CHUNK, tokens.shape[1])
    hidden_act, grad_gateup, back_part, forward_part = call(
        functools.partial(feed_kernel, ff),
        chunks,
        [
            (normed2, row_block, by_row),
            (cotangent, row_block, by_row),
            (last_w, None, None),
        ],
        [
            ((rows, ff), BF16, (CHUNK, ff), by_row),
            ((rows, 2 * ff), BF16, (CHUNK, 2 * ff), by_row),
            (tokens.shape, BF16, row_block, by_row),
            (tokens.shape, BF16, row_block, by_row),
        ],
    )
    grad_norm2 = scatter_rows(back_part)
    grad_values, norm2_part = rms_back(residual, norm2_gain, grad_norm2)
    grad_residual = mine(cotangent, quarter, 0).astype(F32) + grad_values
    late_terms = row_major(
        jnp.concatenate(
            [
                product_tn(normed2, grad_gateup).astype(BF16),
                product_tn(cotangent, hidden_act).astype(BF16),
            ],
            axis=1,
        )
    )
    grad_residual, late_terms = lax.optimization_barrier((grad_residual, late_terms))
    late_grad = lax.psum_scatter(late_terms, WEIGHT_AXES, scatter_dimension=0, tiled=True)
    grad_mix = gather_rows(grad_residual.astype(BF16))
    layer_half = scatter_rows(forward_part, grad_residual, grad_mix)
    layer_q = (residual + layer_half).astype(BF16)

    grad_mixer = product(grad_mix, mixer_w)
    mixer_terms = product_tn(grad_mix, mixer_low).astype(BF16)
    grad_att = grad_mixer[:, :LANES]
    grad_mamba = grad_mixer[:, LANES:]
    grad_y, grad_gate, params_grad, grad_in = call(
        functools.partial(finish_back_kernel, docs, width),
        chunks,
        [
            (meta, "smem", None),
            (grad_mamba, chunk_width, by_row),
            (y, chunk_width, by_row),
            (act, chunk_mix, by_row),
            (cum, chunk_128, by_row),
            (gate_z, chunk_width, by_row),
            (params, None, None),
            (spread, None, None),
            (block_ones, None, None),
        ],
        [
            ((rows, width), F32, chunk_width, by_row),
            ((rows, width), BF16, chunk_width, by_row),
            ((8, width), F32, None, None),
            ((width, NST), F32, None, None),
        ],
        [pltpu.VMEM((8, LANES), F32)],
    )
    grad_ins = gathered(jnp.concatenate([grad_in.astype(BF16), end[width:]], axis=0), "ctx")
    grad_query, grad_kv = call(
        functools.partial(attend_back_kernel, docs),
        blocks,
        [
            (meta, "smem", None),
            (q_rot, block_128, by_row),
            (kv_all, None, None),
            (grad_att, block_128, by_row),
            (attended, block_128, by_row),
            (lse, block_128, by_row),
            (cosine, block_128, by_row),
            (sine, block_128, by_row),
        ],
        [
            ((rows, LANES), BF16, block_128, by_row),
            ((pack, LANES), F32, None, None),
        ],
    )
    grad_kv = scattered(
        grad_kv.astype(BF16).reshape(ctx_size, rows, LANES), "ctx", 0
    ).astype(F32)
    half = HD // 2
    swapped = jnp.concatenate([grad_kv[:, half:HD], grad_kv[:, :half], grad_kv[:, HD:]], axis=1)
    is_key = jnp.arange(LANES)[None, :] < HD
    grad_kv = jnp.where(is_key, grad_kv * cosine - swapped * sine, grad_kv).astype(BF16)
    grad_end = chain(
        grad_ins, range(ctx_size - 1, 0, -1), width, heads, lambda k: k > ctx_rank
    )
    gate_terms = product_tn(normed, jnp.concatenate([grad_gate, grad_query], axis=1)).astype(BF16)
    second_terms = row_major(jnp.concatenate([mixer_terms, gate_terms], axis=1))
    second_terms, grad_end, layer_q = lax.optimization_barrier((second_terms, grad_end, layer_q))
    second_grad = lax.psum_scatter(second_terms, WEIGHT_AXES, scatter_dimension=0, tiled=True)
    layer_out = gather_rows(layer_q)

    def back_row(i):
        return (chunks - 1 - i, 0)

    grad_mixed, grad_step, grad_tail, grad_edge, taps_grad, heads_grad = call(
        functools.partial(scan_back_kernel, docs, width),
        chunks,
        [
            (meta, "smem", None),
            (act, chunk_mix, back_row),
            (slope, chunk_mix, back_row),
            (step, chunk_128, back_row),
            (sig, chunk_128, back_row),
            (cum, chunk_128, back_row),
            (grad_y, chunk_width, back_row),
            (states, (width, NST), back_row),
            (grad_end, None, None),
            (mixed, chunk_mix, back_row),
            (edge, None, None),
            (taps, None, None),
            (head_params, None, None),
            (params, None, None),
            (spread, None, None),
            (spread_t, None, None),
        ],
        [
            ((rows, mix), BF16, chunk_mix, back_row),
            ((rows, LANES), BF16, chunk_128, back_row),
            ((EDGE, mix), F32, None, None),
            ((EDGE, mix), F32, None, None),
            ((8, mix), F32, None, None),
            ((8, LANES), F32, None, None),
        ],
        [pltpu.VMEM((CHUNK + 2 * EDGE, mix), F32), pltpu.VMEM((width, NST), F32)],
    )
    edge_grad = lax.ppermute(grad_edge, "ctx", backward)
    grad_mixed = lax.dynamic_update_slice_in_dim(
        grad_mixed, (grad_tail + edge_grad).astype(BF16), rows - EDGE, 0
    )
    mixed_a = grad_mixed[:, : width + NST]
    mixed_b = jnp.concatenate([grad_mixed[:, width + NST :], grad_kv, grad_step], axis=1)
    grad_all = jnp.concatenate([grad_mixed, grad_query, grad_kv, grad_step, grad_gate], axis=1)
    all_w = jnp.concatenate([first_w, gate_w], axis=1)
    on_chip, finish_rows = scatter_product(grad_all, all_w)
    late_a = Owned(product_tn(normed, after(mixed_a, on_chip)), "ctx")
    late_b = Owned(product_tn(normed, after(mixed_b, on_chip)), "dp")
    late_a.step()
    late_b.step()
    grad_norm1 = finish_rows()
    grad_values, norm1_part = rms_back(hidden_q, norm1_gain, grad_norm1)
    tokens_grad = gather_rows((grad_residual + grad_values).astype(BF16))
    owned_a = late_a.result()
    owned_b = late_b.result()
    kv_owned = owned_b[:, NST : NST + LANES]
    step_grad = owned_b[:, NST + LANES : NST + LANES + heads]
    kv_wide = jnp.concatenate(
        [
            jnp.where(kv_head == head, kv_owned[:, part * HD : (part + 1) * HD], 0.0)
            for part in range(2)
            for head in range(KVH)
        ],
        axis=1,
    )
    shared = jnp.concatenate(
        [kv_wide, owned_a[:, width:], owned_b[:, :NST]], axis=1
    ).astype(BF16)
    shared = after(shared, late_grad)
    late_grad = late_grad.astype(F32)
    gateup_grad = late_grad[:, : 2 * ff].reshape(gateup_proj.shape)
    down_grad = late_grad[:, 2 * ff :].T
    for bit in range(bits_of("tp")):
        other = exchange(shared, "tp", 1 << bit).astype(F32)
        shared = shared.astype(F32) + other
        if bit + 1 < bits_of("tp"):
            shared = shared.astype(BF16)
    keyval_grad = shared[:, : 2 * KVH * HD].reshape(keyval_proj.shape)
    state_grad = shared[:, 2 * KVH * HD :].reshape(state_proj.shape)

    norms = jnp.concatenate([norm1_part.reshape(8, -1), norm2_part.reshape(8, -1)], axis=1)
    small = jnp.concatenate([taps_grad, heads_grad, params_grad, norms], axis=1)
    small = gathered(summed_over(small, ("ctx", "dp")), "tp")
    second_grad = after(second_grad, shared, tokens_grad, small).astype(F32)
    attn_grad = second_grad[:, :LANES].T
    mamba_grad = second_grad[:, LANES : LANES + width].T
    query_grad = second_grad[:, LANES + 2 * width :]
    inner_grad = jnp.concatenate(
        [second_grad[:, LANES + width : LANES + 2 * width], owned_a[:, :width]], axis=1
    ).reshape(inner_proj.shape)
    at = mix + LANES
    convin_grad = small[:, : CONV + 1, :width].transpose(1, 0, 2).reshape(conv_inner.shape)
    stepbias_grad = small[:, 0, mix : mix + heads].reshape(-1)
    decay_grad = small[:, 1, mix : mix + heads].reshape(-1)
    skip_grad = jnp.sum(small[:, 0, at : at + width].reshape(ranks * heads, PD), axis=1)
    mgain_grad = small[:, 1, at : at + width].reshape(-1)
    shared_small = jnp.sum(small, axis=0)
    convst_grad = shared_small[: CONV + 1, width:mix].reshape(conv_state.shape)
    at = at + width
    norm_columns = norm1_part.shape[0] // 8
    norm1_grad = shared_small[:, at : at + norm_columns].reshape(-1)
    norm2_grad = shared_small[:, at + norm_columns :].reshape(-1)
    return (
        layer_out,
        tokens_grad,
        norm1_grad,
        norm2_grad,
        query_grad,
        keyval_grad,
        attn_grad,
        inner_grad,
        state_grad,
        step_grad,
        convin_grad,
        convst_grad,
        stepbias_grad,
        decay_grad,
        skip_grad,
        mgain_grad,
        mamba_grad,
        gateup_grad,
        down_grad,
    )


def solution(mesh):
    rows_split = P(("dp", "ctx"), None)
    split_0 = P(("dp", "ctx"), "tp")
    split_0_whole = P(("dp", "ctx"), None, None)
    split_0_last = P(("dp", "ctx"), None, "tp")
    split_1 = P("tp", ("dp", "ctx"))
    return jax.shard_map(
        body,
        mesh=mesh,
        in_specs=(
            rows_split,
            rows_split,
            P("dp", None),
            P(),
            P(),
            split_0,
            split_0_whole,
            split_1,
            split_0_last,
            split_0_whole,
            split_0,
            P(),
            P(),
            P(),
            P(),
            P(),
            P(),
            split_1,
            split_0_last,
            split_1,
        ),
        out_specs=(
            rows_split,
            rows_split,
            P(),
            P(),
            split_0,
            split_0_whole,
            split_1,
            split_0_last,
            split_0_whole,
            split_0,
            P(),
            P(),
            P(),
            P(),
            P(),
            P(),
            split_1,
            split_0_last,
            split_1,
        ),
        check_vma=False,
    )
```
